256 devices in a mesh: gx: 16 (over z, core), gy: 8 (over y_hi, x), ga: 2 (over y_lo).
Axes of the slice: x: 4, y: 4 (y_hi: 2, y_lo: 2; y = y_hi * 2 + y_lo), z: 8, core: 2. Of those that a mesh axis runs over, the one named last changes fastest.
Arguments:
- euler_table: float32 [3, 2048], replicated, may hold values from -3.140625 to 3.140625
- crystal: float32 [21], replicated, may hold values from -0.08 to 3.4
- orient: int32 [32, 16, 8, 4096], P('ga', 'gx', 'gy'), may hold values from 0 to 2047
- weight: bfloat16 [32, 16, 8, 4096], P('ga', 'gx', 'gy'), may hold values from 0.099609375 to 1
- cell_map: int32 [16, 8, 4096], P('gx', 'gy'), may hold values from 0 to 4095, each once within a row
- density: float32 [256, 128, 16], P('gx', 'gy', 'ga'), may hold values from 0.5 to 2
- velocity: float32 [3, 256, 128, 16], P(None, 'gx', 'gy', 'ga'), may hold values from -6 to 6
- stress: float32 [6, 256, 128, 16], P(None, 'gx', 'gy', 'ga'), may hold values from -6 to 6
Outputs:
- stiffness: float32 [21, 256, 128, 16], P(None, 'gx', 'gy', 'ga')
- final_velocity: float32 [3, 256, 128, 16], P(None, 'gx', 'gy', 'ga')
- final_stress: float32 [6, 256, 128, 16], P(None, 'gx', 'gy', 'ga')
The draws below stay inside these ranges and needn't reach their ends.
Inputs may be any that keep to these rules, and one draw needn't show every extreme that they name: `cell_map`: each partition's row is a permutation of the 4096 canonical indices.
All inputs are finite; a program needn't handle non-finite values.
Results may differ from the reference program's by a relative error of at most 0.0003.
Values sent between devices are 32-bit elements; how exact they have to be, the bound alone decides.
A program may use at most 128 MiB of HBM per device.

```python
import math
import jax
import jax.numpy as jnp
from jax import lax

GRAINS = 32
ORIENTS = 2048
SUB_X = 1
SUB_Y = 2
STEPS = 2
PART_X = 16
PART_Y = 8
NX = 256
NY = 128
NZ = 16
CELLS = 4096


def crystal_ranges():
    lower_ends = []
    upper_ends = []
    for row_index in range(6):
        for col_index in range(row_index, 6):
            if row_index == col_index and row_index < 3:
                lower_ends.append(2.4)
                upper_ends.append(3.4)
            elif row_index == col_index:
                lower_ends.append(0.6)
                upper_ends.append(0.9)
            elif col_index < 3:
                lower_ends.append(0.5)
                upper_ends.append(0.8)
            else:
                lower_ends.append(-0.08)
                upper_ends.append(0.08)
    return (jnp.array(lower_ends, jnp.float32), jnp.array(upper_ends, jnp.float32))


def draw_crystal(key, part):
    lower_ends, upper_ends = crystal_ranges()
    fresh = jax.random.uniform(jax.random.fold_in(key, 11), (21,), jnp.float32)
    return lower_ends + (upper_ends - lower_ends) * fresh


def place_ends(drawn, own_key, least, high):
    longest = drawn.shape.index(max(drawn.shape))
    spots = []
    for shift in (0, 1):
        where = [jax.random.randint(jax.random.fold_in(own_key, axis), (), 0, length) for axis, length in enumerate(drawn.shape)]
        where[longest] = (where[longest] + shift) % drawn.shape[longest]
        spots.append(tuple(where))
    return drawn.at[spots[0]].set(least).at[spots[1]].set(high)


def block_levels(stream_key, shape, split, low, high):
    gain = 1.0
    for axis_at, shards_of in split:
        draws = jax.random.uniform(jax.random.fold_in(jax.random.fold_in(stream_key, 6), axis_at), (shards_of,), jnp.float32, low / len(split), high / len(split))
        gain = gain * jnp.repeat(jnp.exp(draws), shape[axis_at] // shards_of).reshape((-1,) + (1,) * (len(shape) - 1 - axis_at))
    return gain


def centred(stream_key, shape, scale, bound, split=(), kind=jnp.bfloat16):
    drawn = jax.random.normal(stream_key, shape, jnp.float32) * scale
    if len(split) > 0:
        drawn = block_levels(stream_key, shape, split, -0.22, 0.18) * drawn
    return jnp.clip(drawn, min=-bound, max=bound).astype(kind)


def setup_inputs(seed: int = 0) -> dict:
    key_list = jax.random.split(jax.random.key(seed), 9)
    return {
        "euler_table": jnp.clip(jax.random.uniform(key_list[0], (3, ORIENTS), jnp.float32, -3.140625, 3.140625), -3.140625, 3.140625),
        "crystal": draw_crystal(jax.random.fold_in(key_list[8], 71), 0),
        "orient": place_ends(jax.random.randint(key_list[2], (GRAINS, PART_X, PART_Y, CELLS), 0, ORIENTS), jax.random.fold_in(key_list[2], 1), 0, ORIENTS - 1).astype(jnp.int32),
        "weight": jnp.clip(jnp.exp(math.log(1.0) - 2.306499 * jax.random.uniform(key_list[3], (GRAINS, PART_X, PART_Y, CELLS), jnp.float32) ** block_levels(key_list[3], (GRAINS, PART_X, PART_Y, CELLS), ((0, 2), (1, 16), (2, 8)), -0.2, 0.2)), 0.099609375, 1.0).astype(jnp.bfloat16),
        "cell_map": jax.vmap(lambda own: jax.random.permutation(own, CELLS))(jax.random.split(key_list[4], PART_X * PART_Y)).reshape((PART_X, PART_Y, CELLS)).astype(jnp.int32),
        "density": jnp.clip(jnp.exp(math.log(2.0) - 1.3862944 * jax.random.uniform(key_list[5], (NX, NY, NZ), jnp.float32) ** block_levels(key_list[5], (NX, NY, NZ), ((0, 16), (1, 8), (2, 2)), -0.2, 0.2)), 0.5, 2.0),
        "velocity": centred(key_list[6], (3, NX, NY, NZ), 1.0, 6.0, ((1, 16), (2, 8), (3, 2)), jnp.float32),
        "stress": centred(key_list[7], (6, NX, NY, NZ), 1.0, 6.0, ((1, 16), (2, 8), (3, 2)), jnp.float32),
    }


stencil_weights = (0.8, -0.2, 4.0 / 105.0, -1.0 / 280.0)
time_step = 0.2
grain_block = 4
voigt_pairs = ((0, 0), (1, 1), (2, 2), (1, 2), (0, 2), (0, 1))
upper_pairs = [(row_index, col_index) for row_index in range(6) for col_index in range(row_index, 6)]


def symmetric_index(first_index, second_index):
    return upper_pairs.index((min(first_index, second_index), max(first_index, second_index)))


def ordered_sum(summands):
    running = summands[0]
    for summand in summands[1:]:
        running = running + summand
    return running


def rotated_table(euler_table, crystal):
    cos_one, sin_one = jnp.cos(euler_table[0]), jnp.sin(euler_table[0])
    cos_mid, sin_mid = jnp.cos(euler_table[1]), jnp.sin(euler_table[1])
    cos_two, sin_two = jnp.cos(euler_table[2]), jnp.sin(euler_table[2])
    bunge = [[cos_one * cos_two - sin_one * sin_two * cos_mid, sin_one * cos_two + cos_one * sin_two * cos_mid, sin_two * sin_mid],
             [-cos_one * sin_two - sin_one * cos_two * cos_mid, -sin_one * sin_two + cos_one * cos_two * cos_mid, cos_two * sin_mid],
             [sin_one * sin_mid, -cos_one * sin_mid, cos_mid]]
    rotation = [[bunge[col_index][row_index] for col_index in range(3)] for row_index in range(3)]
    bond = []
    for out_index in range(6):
        first, second = voigt_pairs[out_index]
        bond_row = []
        for in_index in range(6):
            third, fourth = voigt_pairs[in_index]
            if in_index < 3:
                bond_row.append(rotation[first][third] * rotation[second][third])
            else:
                bond_row.append(rotation[first][third] * rotation[second][fourth] + rotation[first][fourth] * rotation[second][third])
        bond.append(bond_row)
    entries = [[crystal[symmetric_index(row_index, col_index)] for col_index in range(6)] for row_index in range(6)]
    product = [[ordered_sum([bond[row_index][inner] * entries[inner][col_index] for inner in range(6)]) for col_index in range(6)] for row_index in range(6)]
    rotated = [ordered_sum([product[row_index][inner] * bond[col_index][inner] for inner in range(6)]) for row_index, col_index in upper_pairs]
    return jnp.stack(rotated)


def accumulate(table, orient_rows, weight_rows):
    blocks = orient_rows.shape[0] // grain_block
    count_cells = orient_rows.shape[1]

    def absorb(carry, inputs):
        chosen, masses = inputs
        picked = jnp.take(table, chosen, axis=1)
        masses_wide = masses.astype(jnp.float32)
        return (carry[0] + jnp.sum(picked * masses_wide[None], axis=1), carry[1] + jnp.sum(masses_wide, axis=0)), None

    initial = (jnp.zeros((21, count_cells), jnp.float32), jnp.zeros((count_cells,), jnp.float32))
    result, unused = lax.scan(absorb, initial, (orient_rows.reshape(blocks, grain_block, count_cells), weight_rows.reshape(blocks, grain_block, count_cells)))
    return result


def derivative(padded, direction):
    interior = [padded.shape[0]] + [extent - 8 for extent in padded.shape[1:]]

    def window(offset):
        starts = [0, 4, 4, 4]
        starts[direction] = 4 + offset
        return lax.slice(padded, starts, [begin + extent for begin, extent in zip(starts, interior)])

    result = stencil_weights[0] * (window(1) - window(-1))
    for order_index in range(1, 4):
        result = result + stencil_weights[order_index] * (window(order_index + 1) - window(-order_index - 1))
    return result


def advance_velocity(velocity, padded_stress, density):
    along_x = derivative(jnp.stack([padded_stress[0], padded_stress[5], padded_stress[4]]), 1)
    along_y = derivative(jnp.stack([padded_stress[5], padded_stress[1], padded_stress[3]]), 2)
    along_z = derivative(jnp.stack([padded_stress[4], padded_stress[3], padded_stress[2]]), 3)
    return velocity + time_step * (along_x + along_y + along_z) / density[None]


def advance_stress(stress, padded_velocity, stiffness):
    grad_x = derivative(padded_velocity, 1)
    grad_y = derivative(padded_velocity, 2)
    grad_z = derivative(padded_velocity, 3)
    strain = [grad_x[0], grad_y[1], grad_z[2], grad_y[2] + grad_z[1], grad_x[2] + grad_z[0], grad_x[1] + grad_y[0]]
    updated = []
    for row_index in range(6):
        change = ordered_sum([stiffness[symmetric_index(row_index, col_index)] * strain[col_index] for col_index in range(6)])
        updated.append(stress[row_index] + time_step * change)
    return jnp.stack(updated)


def pad_field(field):
    return jnp.pad(field, ((0, 0), (4, 4), (4, 4), (4, 4)))


def reference(euler_table, crystal, orient, weight, cell_map, density, velocity, stress):
    table = rotated_table(euler_table, crystal)
    partitions = PART_X * PART_Y
    orient_all = orient.reshape(GRAINS, partitions, CELLS)
    weight_all = weight.reshape(GRAINS, partitions, CELLS)
    maps_all = cell_map.reshape(partitions, CELLS)

    def one_part(part_index):
        orient_rows = lax.dynamic_index_in_dim(orient_all, part_index, 1, keepdims=False)
        weight_rows = lax.dynamic_index_in_dim(weight_all, part_index, 1, keepdims=False)
        summed, total = accumulate(table, orient_rows, weight_rows)
        average = summed / total[None]
        slots = lax.dynamic_index_in_dim(maps_all, part_index, 0, keepdims=False)
        return jnp.zeros((21, CELLS), jnp.float32).at[:, slots].set(average)

    placed = lax.map(one_part, jnp.arange(partitions, dtype=jnp.int32))
    placed = placed.reshape(PART_X, PART_Y, 21, PART_X, SUB_X, PART_Y, SUB_Y, NZ)
    stiffness = placed.transpose(2, 3, 0, 4, 5, 1, 6, 7).reshape(21, NX, NY, NZ)
    for step_index in range(STEPS):
        velocity = advance_velocity(velocity, pad_field(stress), density)
        stress = advance_stress(stress, pad_field(velocity), stiffness)
    return (stiffness, velocity, stress)
```

```python
import functools
import math

import jax
import jax.numpy as jnp
from jax import lax
from jax.experimental import pallas as pl
from jax.experimental.pallas import tpu as pltpu
from jax.sharding import PartitionSpec as P

MESH = pl.DeviceIdType.MESH
MERGED = True
STEPS = 2
weights = (0.8, -0.2, 4.0 / 105.0, -1.0 / 280.0)
time_step = 0.2
voigt_pairs = ((0, 0), (1, 1), (2, 2), (1, 2), (0, 2), (0, 1))
upper_pairs = [(row, col) for row in range(6) for col in range(row, 6)]
F32, I32 = jnp.float32, jnp.int32
STRESS_X, STRESS_Y, STRESS_Z = (0, 5, 4), (5, 1, 3), (4, 3, 2)
GX, GY, GA = 16, 8, 2
GRAINS = 16
ROWS = 24
FULL = 32700.0


def upper(first, second):
    return upper_pairs.index((min(first, second), max(first, second)))


def ordered_sum(terms):
    total = terms[0]
    for term in terms[1:]:
        total = total + term
    return total


def lane_pick(row, index):
    return jnp.take_along_axis(row, index, axis=1, mode="promise_in_bounds")


def sublane_pick(block, index):
    return jnp.take_along_axis(block, index, axis=0, mode="promise_in_bounds")


def tree(values, masks):
    for mask in masks:
        values = [
            jnp.where(mask, values[2 * i + 1], values[2 * i]) for i in range(len(values) // 2)
        ]
    return values[0]


def lane_iota(rows):
    return lax.broadcasted_iota(I32, (rows, 128), 1)


def row_iota(rows):
    return lax.broadcasted_iota(I32, (rows, 128), 0)


def rotated_entries(angles, crystal):
    (c1, c0, c2), (s1, s0, s2) = [jnp.cos(a) for a in angles], [jnp.sin(a) for a in angles]
    bunge = [
        [c1 * c2 - s1 * s2 * c0, s1 * c2 + c1 * s2 * c0, s2 * s0],
        [-c1 * s2 - s1 * c2 * c0, -s1 * s2 + c1 * c2 * c0, c2 * s0],
        [s1 * s0, -c1 * s0, c0],
    ]
    rotation = [[bunge[col][row] for col in range(3)] for row in range(3)]
    bond = []
    for i, j in voigt_pairs:
        line = []
        for k, l in voigt_pairs:
            if k == l:
                line.append(rotation[i][k] * rotation[j][k])
            else:
                line.append(rotation[i][k] * rotation[j][l] + rotation[i][l] * rotation[j][k])
        bond.append(line)
    rotated = []
    for row in range(6):
        product = [
            ordered_sum([bond[row][k] * crystal[upper(k, col)] for k in range(6)])
            for col in range(6)
        ]
        for col in range(row, 6):
            rotated.append(ordered_sum([product[k] * bond[col][k] for k in range(6)]))
    return rotated


def prepare(
    euler, crystal, orient, weight, cell_map, angles, entries, table, packed, from_row, from_lane
):
    for j in range(16):
        angles[pl.ds(j, 3, stride=16), :] = euler[:, j * 128 : (j + 1) * 128]
    scalars = [crystal[i] for i in range(21)]
    largest = None
    for half in range(2):
        three = [angles[k * 16 + half * 8 : k * 16 + half * 8 + 8, :] for k in range(3)]
        found = rotated_entries(three, scalars)
        for i, entry in enumerate(found):
            entries[i, half * 8 : half * 8 + 8, :] = entry
            size = jnp.abs(entry)
            largest = size if largest is None else jnp.maximum(largest, size)
    largest = jnp.max(jnp.max(largest, axis=0, keepdims=True), axis=1, keepdims=True)
    largest = jnp.broadcast_to(jnp.maximum(largest, 1e-30), (16, 128))
    scale = FULL / largest
    for pair in range(11):
        high = entries[2 * pair] * scale
        if pair < 10:
            low = jnp.floor(entries[2 * pair + 1] * scale + 0.5)
            high = jnp.floor(high - low * (1.0 / 65536.0) + 0.5).astype(I32)
            table[pair * 16 : pair * 16 + 16, :] = high * 65536 + low.astype(I32)
        else:
            table[pair * 16 : pair * 16 + 16, :] = jnp.floor(high + 0.5).astype(I32) * 65536
    for j in range(32):
        mass = (weight[:, j * 128 : (j + 1) * 128].astype(F32) * 2048.0).astype(I32)
        chosen = orient[pl.ds(j, GRAINS, stride=32), :]
        packed[pl.ds(j, GRAINS, stride=32), :] = chosen * 4096 + mass
    me_x, me_a = lax.axis_index("gx"), lax.axis_index("ga")
    slot = cell_map[...]
    depth = slot & 15
    own = ((depth >> 3) == me_a).astype(I32)
    to_row = own * 16 + (((slot >> 8) - me_x + GX) & 15)
    to_lane = ((slot >> 4) & 15) * 8 + (depth & 7)
    rows, lanes = row_iota(32), row_iota(128)
    here = lane_iota(32).astype(F32)
    found = jnp.zeros((64, 128), F32)
    for j in range(32):
        hit = rows == jnp.broadcast_to(to_row[j : j + 1, :], (32, 128))
        left = jnp.concatenate(
            [jnp.where(hit, float(j), 0.0), jnp.where(hit, here, 0.0)], axis=0
        ).astype(jnp.bfloat16)
        right = jnp.where(lanes == jnp.broadcast_to(to_lane[j : j + 1, :], (128, 128)), 1.0, 0.0)
        found = found + lax.dot_general(
            left,
            right.astype(jnp.bfloat16),
            (((1,), (1,)), ((), ())),
            preferred_element_type=F32,
        )
    found = (found + 0.5).astype(I32)
    from_row[...] = found[:32]
    from_lane[...] = found[32:]
    return largest[:1, :1] * (1.0 / (FULL * 65536.0))


def grain_sums(table, packed, from_row, from_lane, start):
    lane = from_lane[start : start + 8, :]
    row = from_row[start : start + 8, :]
    row_bits = [((row >> bit) & 1) == 1 for bit in range(5)]

    def fetch(grain):
        return tree(
            [
                lane_pick(jnp.broadcast_to(packed[pl.ds(grain * 32 + j, 1), :], (8, 128)), lane)
                for j in range(32)
            ],
            row_bits,
        )

    def absorb(grain, carry):
        word, sums = carry[0], carry[1:]
        following = fetch(jnp.minimum(grain + 1, GRAINS - 1))
        mass = (word & 4095).astype(F32)
        spot = (word >> 12) & 127
        bits = [((word >> (19 + bit)) & 1) == 1 for bit in range(4)]
        out = []
        for pair in range(11):
            value = tree(
                [
                    lane_pick(jnp.broadcast_to(table[pair * 16 + h : pair * 16 + h + 1, :], (8, 128)), spot)
                    for h in range(16)
                ],
                bits,
            )
            out.append(sums[2 * pair] + mass * value.astype(F32))
            if pair < 10:
                out.append(sums[2 * pair + 1] + mass * (value << 16).astype(F32))
        out.append(sums[-1] + mass)
        return (following, *out)

    zero = jnp.zeros((8, 128), F32)
    return lax.fori_loop(0, GRAINS, absorb, (fetch(0),) + (zero,) * 22)[1:]


def block_swap(block, regroup):
    sublane, lane = row_iota(8), lane_iota(8)
    group, place = lane >> 4, lane & 15
    skewed = lane_pick(block, ((group + sublane) & 7) * 16 + place)
    skewed = sublane_pick(skewed, (sublane - group) & 7)
    if regroup:
        y, z = lane & 15, lane >> 4
        group, place = y >> 1, (y & 1) * 8 + z
    return lane_pick(skewed, ((sublane - group) & 7) * 16 + place)


def along_y(field, k, low, high):
    y = lane_iota(16) & 15
    low = pltpu.roll(low, 128 - (4 + 4 * k), 1)
    high = pltpu.roll(high, 16 - 4 * k, 1)
    total = None
    for m in range(1, 5):
        up = pltpu.roll(jnp.where(y < m, high, field), 128 - m, 1)
        down = pltpu.roll(jnp.where(y >= 16 - m, low, field), m, 1)
        term = weights[m - 1] * (up - down)
        total = term if total is None else total + term
    return total


def along_z(field, low, high):
    z = lane_iota(16) >> 4
    total = None
    for m in range(1, 5):
        up = pltpu.roll(jnp.where(z < m, high, field), 128 - 16 * m, 1)
        down = pltpu.roll(jnp.where(z >= 8 - m, low, field), 16 * m, 1)
        term = weights[m - 1] * (up - down)
        total = term if total is None else total + term
    return total


def along_x(padded):
    total = None
    for m in range(1, 5):
        term = weights[m - 1] * (padded[8 + m : 24 + m, :] - padded[8 - m : 24 - m, :])
        total = term if total is None else total + term
    return total


class Halo:
    def __init__(self, step, refs, me):
        self.step, self.me = step, me
        self.xs, self.xl, self.xr, self.xb, self.ys, self.yr, self.zs, self.zr, send, recv = refs
        x, y, a = me
        ends = [((x + 1) % GX, y, a), ((x + GX - 1) % GX, y, a)]
        ends += [(x, (y + 1) % GY, a), (x, (y + GY - 1) % GY, a), (x, y, 1 - a)]
        i = step
        pairs = [
            (self.xs.at[i, :, 8:16], self.xl.at[i]),
            (self.xs.at[i, :, 0:8], self.xr.at[i]),
            (self.ys.at[i, 0], self.yr.at[i, 0]),
            (self.ys.at[i, 1], self.yr.at[i, 1]),
            (self.zs.at[i], self.zr.at[i]),
        ]
        self.copies = [
            pltpu.make_async_remote_copy(
                src_ref=source,
                dst_ref=target,
                send_sem=send.at[i, n],
                recv_sem=recv.at[i, n],
                device_id=end,
                device_id_type=MESH,
            )
            for n, ((source, target), end) in enumerate(zip(pairs, ends))
        ]

    def start(self, along):
        self.fields = along
        fx, fy, fz = along
        i = self.step
        quarter = (lane_iota(16) & 15) >> 2
        for k in range(3):
            self.xs[i, k] = fx[k]
        self.copies[0].start()
        self.copies[1].start()
        for side, offset in ((0, 128 - 12), (1, 0)):
            rolled = [
                pltpu.roll(fy[k], (offset + 4 * k) % 128, 1) if (offset + 4 * k) % 128 else fy[k]
                for k in range(3)
            ]
            self.ys[i, side] = jnp.where(
                quarter == 0, rolled[0], jnp.where(quarter == 1, rolled[1], rolled[2])
            )
            self.copies[2 + side].start()
        for k in range(3):
            self.zs[i, k] = fz[k]
        self.copies[4].start()

    def finish(self):
        x, y, a = self.me
        fx, fy, fz = self.fields
        i = self.step
        for copy in self.copies:
            copy.wait()
        for k in range(3):
            self.xb[k, 0:8, :] = jnp.where(x > 0, self.xl[i, k], 0.0)
            self.xb[k, 8:24, :] = fx[k]
            self.xb[k, 24:32, :] = jnp.where(x < GX - 1, self.xr[i, k], 0.0)
        dx = [along_x(self.xb.at[k]) for k in range(3)]
        low = jnp.where(y > 0, self.yr[i, 0], 0.0)
        high = jnp.where(y < GY - 1, self.yr[i, 1], 0.0)
        dy = [along_y(fy[k], k, low, high) for k in range(3)]
        dz = []
        for k in range(3):
            other = self.zr[i, k]
            dz.append(
                along_z(fz[k], jnp.where(a > 0, other, 0.0), jnp.where(a == 0, other, 0.0))
            )
        return dx, dy, dz


def new_velocity(velocity, diffs, factor):
    dx, dy, dz = diffs
    return [velocity[k] + (dx[k] + dy[k] + dz[k]) * factor for k in range(3)]


def strain_rates(diffs):
    dx, dy, dz = diffs
    return [dx[0], dy[1], dz[2], dy[2] + dz[1], dx[2] + dz[0], dx[1] + dy[0]]


def new_stress(stress, strain, stiffness):
    return [
        stress[row]
        + time_step
        * ordered_sum([stiffness[upper(row, col)] * strain[col] for col in range(6)])
        for row in range(6)
    ]


def stress_parts(stress):
    return tuple([stress[i] for i in which] for which in (STRESS_X, STRESS_Y, STRESS_Z))


def sums_kernel(
    euler, crystal, orient, weight, cell_map, partial, unit, angles, entries, table, packed, row, lane
):
    size = prepare(
        euler, crystal, orient, weight, cell_map, angles, entries, table, packed, row, lane
    )
    unit[...] = jnp.broadcast_to(size, (8, 128))
    for start in (0, 8, 24, 16):
        sums = grain_sums(table, packed, row, lane, start)
        for i in range(22):
            partial[pl.ds(start * ROWS + i, 8, stride=ROWS), :] = sums[i]


def main_kernel(*refs):
    if MERGED:
        euler, crystal, orient, weight, cell_map = refs[:5]
        refs = refs[5:]
    else:
        partial, unit = refs[:2]
        refs = refs[2:]
    density, velocity, stress, stiff_out, velocity_out, stress_out = refs[:6]
    refs = refs[6:]
    if MERGED:
        angles, entries, table, packed, from_row, from_lane, partial = refs[:7]
        refs = refs[7:]
    fields, arrived, first, first_in, second, second_in, stiff = refs[:7]
    rs_send, rs_recv, p1_send, p1_recv, p2_send, p2_recv = refs[7:13]
    halo_refs = refs[13:]

    x, y, a = lax.axis_index("gx"), lax.axis_index("gy"), lax.axis_index("ga")
    barrier = pltpu.get_barrier_semaphore()
    ends = [((x + d) % GX, y, a) for d in range(1, GX)]
    ends += [(x, (y + d) % GY, a) for d in range(1, GY)]
    ends += [(x, y, 1 - a)]
    for end in ends:
        pl.semaphore_signal(barrier, inc=1, device_id=end, device_id_type=MESH)

    for z in range(8):
        lanes = slice(z * 16, z * 16 + 16)
        fields[0:96, lanes] = stress[pl.ds(z, 96, stride=8), :]
        fields[96:144, lanes] = velocity[pl.ds(z, 48, stride=8), :]
        fields[144:160, lanes] = density[pl.ds(z, 16, stride=8), :]
    stresses = [fields[i * 16 : i * 16 + 16, :] for i in range(6)]
    pl.semaphore_wait(barrier, len(ends))

    halos = [Halo(step, halo_refs, (x, y, a)) for step in range(2 * STEPS)]
    halos[0].start(stress_parts(stresses))

    half = [
        pltpu.make_async_remote_copy(
            src_ref=partial.at[pl.ds(i * 8 * ROWS, 8 * ROWS), :],
            dst_ref=arrived.at[pl.ds(i * 8 * ROWS, 8 * ROWS), :],
            send_sem=rs_send.at[i],
            recv_sem=rs_recv.at[i],
            device_id=(x, y, 1 - a),
            device_id_type=MESH,
        )
        for i in range(2)
    ]

    if MERGED:
        size = prepare(
            euler, crystal, orient, weight, cell_map,
            angles, entries, table, packed, from_row, from_lane,
        )
    else:
        half[0].start()
        half[1].start()
        size = unit[:1, :1]

    factor = time_step / fields[144:160, :]
    velocities = [fields[96 + k * 16 : 112 + k * 16, :] for k in range(3)]
    velocities = new_velocity(velocities, halos[0].finish(), factor)
    for k in range(3):
        fields[96 + k * 16 : 112 + k * 16, :] = velocities[k]
    halos[1].start((velocities,) * 3)

    def sums_of(start):
        if MERGED:
            return grain_sums(table, packed, from_row, from_lane, start)
        return [partial[pl.ds(start * ROWS + i, 8, stride=ROWS), :] for i in range(22)]

    if MERGED:
        for i in range(2):
            sums = sums_of(i * 8)
            for c in range(22):
                partial[pl.ds(i * 8 * ROWS + c, 8, stride=ROWS), :] = sums[c]
            half[i].start()
    strain = strain_rates(halos[1].finish())
    for i in range(6):
        fields[144 + i * 16 : 160 + i * 16, :] = strain[i]

    to_brick = [None] * GX
    for d in range(1, GX):
        to_brick[d] = pltpu.make_async_remote_copy(
            src_ref=first.at[pl.ds(d * ROWS, ROWS), :],
            dst_ref=first_in.at[x],
            send_sem=p1_send.at[d - 1],
            recv_sem=p1_recv.at[d - 1],
            device_id=((x + d) % GX, y, a),
            device_id_type=MESH,
        )
    for i in (1, 0):
        sums = sums_of(16 + i * 8)
        half[i].wait()
        base = i * 8 * ROWS
        total = sums[21] + arrived[pl.ds(base + 21, 8, stride=ROWS), :]
        gain = jnp.broadcast_to(size, (8, 128)) / total
        for c in range(21):
            both = sums[c] + arrived[pl.ds(base + c, 8, stride=ROWS), :]
            first[pl.ds(base + c, 8, stride=ROWS), :] = both * gain
        for d in range(i * 8, i * 8 + 8):
            if d:
                to_brick[d].start()
    first_in[x] = first[0:ROWS, :]
    for d in range(1, GX):
        to_brick[d].wait()

    for p in range(2):
        for c in range(21):
            block = first_in[p * 8 : p * 8 + 8, c, :]
            second[pl.ds(p * ROWS + c, 8, stride=2 * ROWS), :] = block_swap(block, False)
    to_y = []
    for d in range(1, GY):
        target = (y + d) % GY
        copy = pltpu.make_async_remote_copy(
            src_ref=second.at[pl.ds(pl.multiple_of(target * 2 * ROWS, 8), 2 * ROWS), :],
            dst_ref=second_in.at[y],
            send_sem=p2_send.at[d - 1],
            recv_sem=p2_recv.at[d - 1],
            device_id=(x, target, a),
            device_id_type=MESH,
        )
        copy.start()
        to_y.append(copy)
    second_in[y] = second[pl.ds(pl.multiple_of(y * 2 * ROWS, 8), 2 * ROWS), :]
    for copy in to_y:
        copy.wait()
    for p in range(2):
        for c in range(21):
            block = second_in[:, p * ROWS + c, :]
            stiff[c, p * 8 : p * 8 + 8, :] = block_swap(block, True)

    strain = [fields[144 + i * 16 : 160 + i * 16, :] for i in range(6)]
    stresses = [fields[i * 16 : i * 16 + 16, :] for i in range(6)]
    stresses = new_stress(stresses, strain, stiff)
    halos[2].start(stress_parts(stresses))
    for r in range(8):
        for p in range(2):
            turned = jnp.transpose(second_in[r, p * ROWS : p * ROWS + ROWS, :], (1, 0))
            for q in range(8):
                row = ((p * 8 + q) * 16 + 2 * r) * 8
                stiff_out[row : row + 16, :] = turned[q * 16 : q * 16 + 16, :21]
    velocities = new_velocity(velocities, halos[2].finish(), factor)
    halos[3].start((velocities,) * 3)
    for k in range(3):
        for z in range(8):
            velocity_out[pl.ds(k * 128 + z, 16, stride=8), :] = velocities[k][:, z * 16 : z * 16 + 16]
    strain = strain_rates(halos[3].finish())
    stresses = new_stress(stresses, strain, stiff)
    for k in range(6):
        for z in range(8):
            stress_out[pl.ds(k * 128 + z, 16, stride=8), :] = stresses[k][:, z * 16 : z * 16 + 16]


def on_device(euler_table, crystal, orient, weight, cell_map, density, velocity, stress):
    vmem, smem = pl.BlockSpec(memory_space=pltpu.VMEM), pl.BlockSpec(memory_space=pltpu.SMEM)
    grains = (
        euler_table,
        crystal,
        orient.reshape(512, 128),
        weight.reshape(GRAINS, 4096),
        cell_map.reshape(32, 128),
    )
    grain_specs = [vmem, smem, vmem, vmem, vmem]
    grain_scratch = [
        pltpu.VMEM((48, 128), F32),
        pltpu.VMEM((21, 16, 128), F32),
        pltpu.VMEM((176, 128), I32),
        pltpu.VMEM((512, 128), I32),
        pltpu.VMEM((32, 128), I32),
        pltpu.VMEM((32, 128), I32),
    ]
    waves = (
        density.transpose(0, 2, 1).reshape(128, 16),
        velocity.transpose(0, 1, 3, 2).reshape(384, 16),
        stress.transpose(0, 1, 3, 2).reshape(768, 16),
    )
    if MERGED:
        operands, specs = grains, grain_specs
        scratch = grain_scratch + [pltpu.VMEM((16 * ROWS, 128), F32)]
    else:
        operands = pl.pallas_call(
            sums_kernel,
            out_shape=(
                jax.ShapeDtypeStruct((32 * ROWS, 128), F32),
                jax.ShapeDtypeStruct((8, 128), F32),
            ),
            in_specs=grain_specs,
            out_specs=(vmem, vmem),
            scratch_shapes=grain_scratch,
            name="grain_sums",
        )(*grains)
        specs, scratch = [vmem, vmem], []
    scratch = scratch + [
        pltpu.VMEM((240, 128), F32),
        pltpu.VMEM((16 * ROWS, 128), F32),
        pltpu.VMEM((16 * ROWS, 128), F32),
        pltpu.VMEM((16, ROWS, 128), F32),
        pltpu.VMEM((16 * ROWS, 128), F32),
        pltpu.VMEM((8, 2 * ROWS, 128), F32),
        pltpu.VMEM((21, 16, 128), F32),
    ]
    for count in (2, 2, 15, 15, 7, 7):
        scratch.append(pltpu.SemaphoreType.DMA((count,)))
    steps = 2 * STEPS
    scratch += [
        pltpu.VMEM((steps, 3, 16, 128), F32),
        pltpu.VMEM((steps, 3, 8, 128), F32),
        pltpu.VMEM((steps, 3, 8, 128), F32),
        pltpu.VMEM((3, 32, 128), F32),
        pltpu.VMEM((steps, 2, 16, 128), F32),
        pltpu.VMEM((steps, 2, 16, 128), F32),
        pltpu.VMEM((steps, 3, 16, 128), F32),
        pltpu.VMEM((steps, 3, 16, 128), F32),
        pltpu.SemaphoreType.DMA((steps, 5)),
        pltpu.SemaphoreType.DMA((steps, 5)),
    ]
    stiffness, velocity, stress = pl.pallas_call(
        main_kernel,
        out_shape=(
            jax.ShapeDtypeStruct((2048, 21), F32),
            jax.ShapeDtypeStruct((384, 16), F32),
            jax.ShapeDtypeStruct((768, 16), F32),
        ),
        in_specs=list(specs) + [vmem, vmem, vmem],
        out_specs=(vmem, vmem, vmem),
        scratch_shapes=scratch,
        compiler_params=pltpu.CompilerParams(
            collective_id=0, has_side_effects=True, vmem_limit_bytes=32 * 1024 * 1024
        ),
        name="relay_and_steps",
    )(*operands, *waves)
    return (
        stiffness.reshape(16, 16, 8, 21).transpose(3, 0, 1, 2),
        velocity.reshape(3, 16, 8, 16).transpose(0, 1, 3, 2),
        stress.reshape(6, 16, 8, 16).transpose(0, 1, 3, 2),
    )


def solution(mesh):
    fields = P(None, "gx", "gy", "ga")
    return jax.shard_map(
        on_device,
        mesh=mesh,
        in_specs=(
            P(),
            P(),
            P("ga", "gx", "gy", None),
            P("ga", "gx", "gy", None),
            P("gx", "gy", None),
            P("gx", "gy", "ga"),
            fields,
            fields,
        ),
        out_specs=(fields, fields, fields),
        check_vma=False,
    )
```

```python
import jax
import jax.numpy as jnp
import numpy as np
from jax import lax
from jax.experimental import pallas as pl
from jax.experimental.pallas import tpu as pltpu
from jax.sharding import PartitionSpec as P

MESH = pl.DeviceIdType.MESH
STEPS = 2
weights = (0.8, -0.2, 4.0 / 105.0, -1.0 / 280.0)
time_step = 0.2
voigt_pairs = ((0, 0), (1, 1), (2, 2), (1, 2), (0, 2), (0, 1))
upper_pairs = [(row, col) for row in range(6) for col in range(row, 6)]
F32, I32 = jnp.float32, jnp.int32
STRESS_X, STRESS_Y, STRESS_Z = (0, 5, 4), (5, 1, 3), (4, 3, 2)
GX, GY, GA = 16, 8, 2
GRAINS = 16
PARTS = 19
ROWS = 24
FULL = 32767.0
NEAR = 4


def upper(first, second):
    return upper_pairs.index((min(first, second), max(first, second)))


def ordered_sum(terms):
    total = terms[0]
    for term in terms[1:]:
        total = total + term
    return total


def entry_map(rotation):
    bond = np.zeros((6, 6))
    for i, (p, q) in enumerate(voigt_pairs):
        for j, (k, l) in enumerate(voigt_pairs):
            bond[i, j] = rotation[p, k] * rotation[q, l]
            if k != l:
                bond[i, j] += rotation[p, l] * rotation[q, k]
    image = np.zeros((21, 21))
    for n, (row, col) in enumerate(upper_pairs):
        unit = np.zeros((6, 6))
        unit[row, col] = unit[col, row] = 1.0
        turned = bond @ unit @ bond.T
        image[:, n] = [turned[i, j] for i, j in upper_pairs]
    return image


def turn(axis, angle):
    i, j = (axis + 1) % 3, (axis + 2) % 3
    out = np.eye(3)
    out[i, i] = out[j, j] = np.cos(angle)
    out[j, i] = np.sin(angle)
    out[i, j] = -out[j, i]
    return out


def harmonic_parts():
    size = np.sqrt([(1.0 + (r > 2)) * (1 + (c > 2)) * (1 + (r != c)) for r, c in upper_pairs])
    spins = []
    for axis in range(3):
        spin = np.zeros((21, 21))
        for n in range(16):
            angle = 2 * np.pi * n / 16
            image = size[:, None] * entry_map(turn(axis, angle)) / size
            spin += sum(m * np.sin(m * angle) for m in range(1, 5)) / 8 * image
        spins.append(spin)
    unit = np.eye(21)
    square = -(spins[0] @ spins[0] + spins[1] @ spins[1] + spins[2] @ spins[2])
    level = spins[2] @ spins[2]
    flat = unit
    for m in range(1, 5):
        flat = flat @ (unit + level / m**2)
    chosen = {0: (0, 1), 2: (upper(2, 2), upper(0, 1)), 4: (upper(2, 2),)}
    parts = []
    for degree, seeds in chosen.items():
        keep = flat
        for other in (0, 2, 4):
            if other != degree:
                first, last = degree * (degree + 1), other * (other + 1)
                keep = keep @ (square - last * unit) / (first - last)
        heads = []
        for seed in seeds:
            head = keep[:, seed]
            for former in heads:
                head = head - former * (former @ head)
            heads.append(head / np.linalg.norm(head))
            chain = [heads[-1]]
            for m in range(degree):
                step = spins[1] @ chain[m]
                if m:
                    step = step - chain[m - 1] * (chain[m - 1] @ step)
                chain.append(step / np.linalg.norm(step))
            part = [chain[0]]
            for m in range(1, degree + 1):
                part += [chain[m], spins[2] @ chain[m] / m]
            parts.append(np.stack(part, axis=1))
    basis = np.concatenate(parts[2:], axis=1)
    even = np.concatenate(parts[:2], axis=1)
    quarter = basis.T @ (size[:, None] * entry_map(turn(1, np.pi / 2)) / size) @ basis
    tables = (basis.T * size, basis / size[:, None], (even @ even.T) / size[:, None] * size, quarter)
    return [np.round(table, 9) for table in tables]


TO_PARTS, FROM_PARTS, EVEN, QUARTER = harmonic_parts()
BLOCKS = ((0, 2), (5, 2), (10, 4))


def sparse(row, values):
    terms = []
    for k in range(len(values)):
        factor = float(row[k])
        if factor:
            terms.append(values[k] if factor == 1 else -values[k] if factor == -1 else factor * values[k])
    return ordered_sum(terms) if terms else None


def quarter_turn(parts, matrix):
    out = []
    for start, degree in BLOCKS:
        stop = start + 2 * degree + 1
        out += [sparse(matrix[i, start:stop], parts[start:stop]) for i in range(start, stop)]
    return out


def about_z(parts, cos, sin):
    out = []
    for start, degree in BLOCKS:
        out.append(parts[start] if cos[0] is None else parts[start] * cos[0])
        for m in range(1, degree + 1):
            a, b = parts[start + 2 * m - 1], parts[start + 2 * m]
            out += [a * cos[m] - b * sin[m], a * sin[m] + b * cos[m]]
    return out


def multiples(cos, sin):
    twice = cos + cos
    cos, sin = [None, cos, twice * cos - 1.0], [None, sin, twice * sin]
    for m in (3, 4):
        cos.append(twice * cos[m - 1] - cos[m - 2])
        sin.append(twice * sin[m - 1] - sin[m - 2])
    return cos, sin


def lane_pick(row, index):
    return jnp.take_along_axis(row, index, axis=1, mode="promise_in_bounds")


def sublane_pick(block, index):
    return jnp.take_along_axis(block, index, axis=0, mode="promise_in_bounds")


def tree(values, masks):
    for mask in masks:
        values = [
            jnp.where(mask, values[2 * i + 1], values[2 * i]) for i in range(len(values) // 2)
        ]
    return values[0]


def lane_iota(rows):
    return lax.broadcasted_iota(I32, (rows, 128), 1)


def row_iota(rows):
    return lax.broadcasted_iota(I32, (rows, 128), 0)


def pair_word(first, second):
    low = jnp.floor(second * FULL + 0.5)
    high = jnp.floor(first * FULL - low * (1.0 / 65536.0) + 0.5).astype(I32)
    return high * 65536 + low.astype(I32)


def prepare_table(euler, crystal, angles, table, seeds, even):
    for j in range(16):
        angles[pl.ds(j, 3, stride=16), :] = euler[:, j * 128 : (j + 1) * 128]
    for k in range(3):
        angle = angles[k * 16 : k * 16 + 16, :]
        table[k * 16 : k * 16 + 16, :] = pair_word(jnp.cos(angle), jnp.sin(angle))
    values = [jnp.full((8, 128), crystal[i], F32) for i in range(21)]
    for i in range(PARTS):
        seeds[i] = sparse(TO_PARTS[i], values)
    for i in range(21):
        found = sparse(EVEN[i], values)
        even[i] = jnp.zeros((8, 128), F32) if found is None else found


def prepare_cells(orient, weight, cell_map, packed, from_row, from_lane):
    for j in range(32):
        mass = (weight[:, j * 128 : (j + 1) * 128].astype(F32) * 2048.0).astype(I32)
        chosen = orient[pl.ds(j, GRAINS, stride=32), :]
        packed[pl.ds(j, GRAINS, stride=32), :] = chosen * 4096 + mass
    me_x, me_a = lax.axis_index("gx"), lax.axis_index("ga")
    slot = cell_map[...]
    depth = slot & 15
    own = ((depth >> 3) == me_a).astype(I32)
    to_row = own * 16 + (((slot >> 8) - me_x + (GX - NEAR)) & 15)
    to_lane = ((slot >> 4) & 15) * 8 + (depth & 7)
    rows, lanes = row_iota(32), row_iota(128)
    here = lane_iota(32).astype(F32)
    found = jnp.zeros((64, 128), F32)
    for j in range(32):
        hit = rows == jnp.broadcast_to(to_row[j : j + 1, :], (32, 128))
        left = jnp.concatenate(
            [jnp.where(hit, float(j), 0.0), jnp.where(hit, here, 0.0)], axis=0
        ).astype(jnp.bfloat16)
        right = jnp.where(lanes == jnp.broadcast_to(to_lane[j : j + 1, :], (128, 128)), 1.0, 0.0)
        found = found + lax.dot_general(
            left,
            right.astype(jnp.bfloat16),
            (((1,), (1,)), ((), ())),
            preferred_element_type=F32,
        )
    found = (found + 0.5).astype(I32)
    from_row[...] = found[:32]
    from_lane[...] = found[32:]


def grain_sums(table, seeds, packed, from_row, from_lane, start):
    lane = from_lane[start : start + 8, :]
    row = from_row[start : start + 8, :]
    row_bits = [((row >> bit) & 1) == 1 for bit in range(5)]

    def fetch(grain):
        return tree(
            [
                lane_pick(jnp.broadcast_to(packed[pl.ds(grain * 32 + j, 1), :], (8, 128)), lane)
                for j in range(32)
            ],
            row_bits,
        )

    def angles_of(word):
        spot = (word >> 12) & 127
        bits = [((word >> (19 + bit)) & 1) == 1 for bit in range(4)]
        return [
            tree(
                [
                    lane_pick(
                        jnp.broadcast_to(table[k * 16 + h : k * 16 + h + 1, :], (8, 128)), spot
                    )
                    for h in range(16)
                ],
                bits,
            )
            for k in range(3)
        ]

    def absorb(grain, carry):
        word, pairs, sums = carry[0], carry[1:4], carry[4:]
        coming = carry[0 + 4 + PARTS + 1]
        sums = sums[: PARTS + 1]
        after = fetch(jnp.minimum(grain + 2, GRAINS - 1))
        coming_pairs = angles_of(coming)
        mass = (word & 4095).astype(F32)
        unit = 1.0 / (FULL * 65536.0)
        turns = [
            multiples(pair.astype(F32) * unit, (pair << 16).astype(F32) * unit) for pair in pairs
        ]
        cos, sin = turns[2]
        cos = [mass] + [mass * value for value in cos[1:]]
        sin = [None] + [mass * value for value in sin[1:]]
        parts = about_z([seeds[i] for i in range(PARTS)], cos, sin)
        parts = quarter_turn(parts, QUARTER.T)
        parts = about_z(parts, *turns[1])
        parts = quarter_turn(parts, QUARTER)
        parts = about_z(parts, *turns[0])
        out = [old + new for old, new in zip(sums, parts)] + [sums[PARTS] + mass]
        return (coming, *coming_pairs, *out, after)

    zero = jnp.zeros((8, 128), F32)
    first, second = fetch(0), fetch(1)
    carry = (first, *angles_of(first)) + (zero,) * (PARTS + 1) + (second,)
    return lax.fori_loop(0, GRAINS, absorb, carry)[4 : 4 + PARTS + 1]


def block_swap(block, regroup):
    sublane, lane = row_iota(8), lane_iota(8)
    group, place = lane >> 4, lane & 15
    skewed = lane_pick(block, ((group + sublane) & 7) * 16 + place)
    skewed = sublane_pick(skewed, (sublane - group) & 7)
    if regroup:
        y, z = lane & 15, lane >> 4
        group, place = y >> 1, (y & 1) * 8 + z
    return lane_pick(skewed, ((sublane - group) & 7) * 16 + place)


def along_y(field, k, low, high):
    y = lane_iota(16) & 15
    low = pltpu.roll(low, 128 - (4 + 4 * k), 1)
    high = pltpu.roll(high, 16 - 4 * k, 1)
    total = None
    for m in range(1, 5):
        up = pltpu.roll(jnp.where(y < m, high, field), 128 - m, 1)
        down = pltpu.roll(jnp.where(y >= 16 - m, low, field), m, 1)
        term = weights[m - 1] * (up - down)
        total = term if total is None else total + term
    return total


def along_z(field, low, high):
    z = lane_iota(16) >> 4
    total = None
    for m in range(1, 5):
        up = pltpu.roll(jnp.where(z < m, high, field), 128 - 16 * m, 1)
        down = pltpu.roll(jnp.where(z >= 8 - m, low, field), 16 * m, 1)
        term = weights[m - 1] * (up - down)
        total = term if total is None else total + term
    return total


def along_x(padded):
    total = None
    for m in range(1, 5):
        term = weights[m - 1] * (padded[8 + m : 24 + m, :] - padded[8 - m : 24 - m, :])
        total = term if total is None else total + term
    return total


class Halo:
    def __init__(self, step, refs, me):
        self.step, self.me = step, me
        self.xs, self.xl, self.xr, self.xb, self.ys, self.yr, self.zs, self.zr, send, recv = refs
        x, y, a = me
        ends = [((x + 1) % GX, y, a), ((x + GX - 1) % GX, y, a)]
        ends += [(x, (y + 1) % GY, a), (x, (y + GY - 1) % GY, a), (x, y, 1 - a)]
        i = step
        pairs = [
            (self.xs.at[i, :, 8:16], self.xl.at[i]),
            (self.xs.at[i, :, 0:8], self.xr.at[i]),
            (self.ys.at[i, 0], self.yr.at[i, 0]),
            (self.ys.at[i, 1], self.yr.at[i, 1]),
            (self.zs.at[i], self.zr.at[i]),
        ]
        self.copies = [
            pltpu.make_async_remote_copy(
                src_ref=source,
                dst_ref=target,
                send_sem=send.at[i, n],
                recv_sem=recv.at[i, n],
                device_id=end,
                device_id_type=MESH,
            )
            for n, ((source, target), end) in enumerate(zip(pairs, ends))
        ]

    def start(self, along):
        self.fields = along
        fx, fy, fz = along
        i = self.step
        quarter = (lane_iota(16) & 15) >> 2
        for k in range(3):
            self.xs[i, k] = fx[k]
        self.copies[0].start()
        self.copies[1].start()
        for side, offset in ((0, 128 - 12), (1, 0)):
            rolled = [
                pltpu.roll(fy[k], (offset + 4 * k) % 128, 1) if (offset + 4 * k) % 128 else fy[k]
                for k in range(3)
            ]
            self.ys[i, side] = jnp.where(
                quarter == 0, rolled[0], jnp.where(quarter == 1, rolled[1], rolled[2])
            )
            self.copies[2 + side].start()
        for k in range(3):
            self.zs[i, k] = fz[k]
        self.copies[4].start()

    def finish(self):
        x, y, a = self.me
        fx, fy, fz = self.fields
        i = self.step
        for copy in self.copies:
            copy.wait()
        for k in range(3):
            self.xb[k, 0:8, :] = jnp.where(x > 0, self.xl[i, k], 0.0)
            self.xb[k, 8:24, :] = fx[k]
            self.xb[k, 24:32, :] = jnp.where(x < GX - 1, self.xr[i, k], 0.0)
        dx = [along_x(self.xb.at[k]) for k in range(3)]
        low = jnp.where(y > 0, self.yr[i, 0], 0.0)
        high = jnp.where(y < GY - 1, self.yr[i, 1], 0.0)
        dy = [along_y(fy[k], k, low, high) for k in range(3)]
        dz = []
        for k in range(3):
            other = self.zr[i, k]
            dz.append(
                along_z(fz[k], jnp.where(a > 0, other, 0.0), jnp.where(a == 0, other, 0.0))
            )
        return dx, dy, dz


def new_velocity(velocity, diffs, factor):
    dx, dy, dz = diffs
    return [velocity[k] + (dx[k] + dy[k] + dz[k]) * factor for k in range(3)]


def strain_rates(diffs):
    dx, dy, dz = diffs
    return [dx[0], dy[1], dz[2], dy[2] + dz[1], dx[2] + dz[0], dx[1] + dy[0]]


def new_stress(stress, strain, stiffness):
    return [
        stress[row]
        + time_step
        * ordered_sum([stiffness[upper(row, col)] * strain[col] for col in range(6)])
        for row in range(6)
    ]


def stress_parts(stress):
    return tuple([stress[i] for i in which] for which in (STRESS_X, STRESS_Y, STRESS_Z))


def entries_of(parts, even):
    out = []
    for i in range(21):
        entry = sparse(FROM_PARTS[i], parts)
        if EVEN[i].any():
            constant = jnp.concatenate([even[i], even[i]], axis=0)
            entry = constant if entry is None else entry + constant
        out.append(entry)
    return out


def main_kernel(*refs):
    given, outs, refs = refs[:8], refs[8:11], refs[11:]
    stiff_out, velocity_out, stress_out = outs
    held, refs = refs[:8], refs[8:]
    angles, table, seeds, even, packed, from_row, from_lane, partial = refs[:8]
    refs = refs[8:]
    fields, arrived, first, first_in, second, second_in, stiff, load_sem = refs[:8]
    rs_send, rs_recv, p1_send, p1_recv, p2_send, p2_recv = refs[8:14]
    halo_refs = refs[14:]

    loads = [pltpu.make_async_copy(given[i], held[i], load_sem.at[i]) for i in range(8)]
    for load in loads:
        load.start()
    euler, crystal, orient, weight, cell_map, density, velocity, stress = held
    x, y, a = lax.axis_index("gx"), lax.axis_index("gy"), lax.axis_index("ga")
    barrier = pltpu.get_barrier_semaphore()
    ends = [((x + d) % GX, y, a) for d in range(1, GX)]
    ends += [(x, (y + d) % GY, a) for d in range(1, GY)]
    ends += [(x, y, 1 - a)]
    for end in ends:
        pl.semaphore_signal(barrier, inc=1, device_id=end, device_id_type=MESH)

    for i in range(5):
        loads[i].wait()
    prepare_table(euler, crystal, angles, table, seeds, even)
    prepare_cells(orient, weight, cell_map, packed, from_row, from_lane)

    halos = [Halo(step, halo_refs, (x, y, a)) for step in range(2 * STEPS)]
    half = [
        pltpu.make_async_remote_copy(
            src_ref=partial.at[pl.ds(i * 8, 8), 0 : PARTS + 1],
            dst_ref=arrived.at[pl.ds(i * 8, 8), 0 : PARTS + 1],
            send_sem=rs_send.at[i],
            recv_sem=rs_recv.at[i],
            device_id=(x, y, 1 - a),
            device_id_type=MESH,
        )
        for i in range(2)
    ]
    to_brick = {}
    for row in range(16):
        d = (row + NEAR) % GX
        if d:
            to_brick[row] = pltpu.make_async_remote_copy(
                src_ref=first.at[row, 0:PARTS],
                dst_ref=first_in.at[x, 0:PARTS],
                send_sem=p1_send.at[d - 1],
                recv_sem=p1_recv.at[d - 1],
                device_id=((x + d) % GX, y, a),
                device_id_type=MESH,
            )

    def sums_of(start):
        return grain_sums(table, seeds, packed, from_row, from_lane, start)

    def other_half(i):
        sums = sums_of(i * 8)
        for c in range(PARTS + 1):
            partial[i * 8 : i * 8 + 8, c, :] = sums[c]

    def own_half(i):
        sums = sums_of(16 + i * 8)
        half[i].wait()
        rows = slice(i * 8, i * 8 + 8)
        gain = 1.0 / (sums[PARTS] + arrived[rows, PARTS, :])
        for c in range(PARTS):
            first[rows, c, :] = (sums[c] + arrived[rows, c, :]) * gain
        for row in range(i * 8, i * 8 + 8):
            if row in to_brick:
                to_brick[row].start()

    other_half(0)
    for i in range(5, 8):
        loads[i].wait()
    for z in range(8):
        lanes = slice(z * 16, z * 16 + 16)
        fields[0:96, lanes] = stress[pl.ds(z, 96, stride=8), :]
        fields[96:144, lanes] = velocity[pl.ds(z, 48, stride=8), :]
        fields[144:160, lanes] = density[pl.ds(z, 16, stride=8), :]
    stresses = [fields[i * 16 : i * 16 + 16, :] for i in range(6)]
    pl.semaphore_wait(barrier, len(ends))
    half[0].start()
    halos[0].start(stress_parts(stresses))
    other_half(1)
    half[1].start()
    own_half(0)
    factor = time_step / fields[144:160, :]
    velocities = [fields[96 + k * 16 : 112 + k * 16, :] for k in range(3)]
    velocities = new_velocity(velocities, halos[0].finish(), factor)
    for k in range(3):
        fields[96 + k * 16 : 112 + k * 16, :] = velocities[k]
    fields[144:160, :] = factor
    halos[1].start((velocities,) * 3)
    own_half(1)
    velocities = [fields[96 + k * 16 : 112 + k * 16, :] for k in range(3)]
    halos[1].fields = (velocities,) * 3
    strain = strain_rates(halos[1].finish())
    for i in range(6):
        fields[160 + i * 16 : 176 + i * 16, :] = strain[i]
    first_in[x, 0:PARTS, :] = first[GX - NEAR, 0:PARTS, :]
    for copy in to_brick.values():
        copy.wait()

    for p in range(2):
        for c in range(PARTS):
            block = first_in[p * 8 : p * 8 + 8, c, :]
            second[:, p, c, :] = block_swap(block, False)
    to_y = []
    for d in range(1, GY):
        target = (y + d) % GY
        copy = pltpu.make_async_remote_copy(
            src_ref=second.at[target, :, 0:PARTS],
            dst_ref=second_in.at[y, :, 0:PARTS],
            send_sem=p2_send.at[d - 1],
            recv_sem=p2_recv.at[d - 1],
            device_id=(x, target, a),
            device_id_type=MESH,
        )
        copy.start()
        to_y.append(copy)
    for p in range(2):
        second_in[y, p, 0:PARTS, :] = second[y, p, 0:PARTS, :]
    for copy in to_y:
        copy.wait()
    parts = []
    for c in range(PARTS):
        parts.append(
            jnp.concatenate([block_swap(second_in[:, p, c, :], True) for p in range(2)], axis=0)
        )
    for i, entry in enumerate(entries_of(parts, even)):
        stiff[i] = entry

    strain = [fields[160 + i * 16 : 176 + i * 16, :] for i in range(6)]
    stresses = [fields[i * 16 : i * 16 + 16, :] for i in range(6)]
    stresses = new_stress(stresses, strain, stiff)
    halos[2].start(stress_parts(stresses))
    for row in range(16):
        turned = jnp.transpose(stiff[:, row, :], (1, 0))
        for z in range(8):
            stiff_out[pl.ds(row * 128 + z, 16, stride=8), :] = turned[z * 16 : z * 16 + 16, :21]
    factor = fields[144:160, :]
    velocities = [fields[96 + k * 16 : 112 + k * 16, :] for k in range(3)]
    velocities = new_velocity(velocities, halos[2].finish(), factor)
    halos[3].start((velocities,) * 3)
    for k in range(3):
        for z in range(8):
            velocity_out[pl.ds(k * 128 + z, 16, stride=8), :] = velocities[k][:, z * 16 : z * 16 + 16]
    strain = strain_rates(halos[3].finish())
    stresses = new_stress(stresses, strain, stiff)
    for k in range(6):
        for z in range(8):
            stress_out[pl.ds(k * 128 + z, 16, stride=8), :] = stresses[k][:, z * 16 : z * 16 + 16]


def on_device(euler_table, crystal, orient, weight, cell_map, density, velocity, stress):
    anywhere, vmem = pl.BlockSpec(memory_space=pl.ANY), pl.BlockSpec(memory_space=pltpu.VMEM)
    operands = (
        euler_table,
        crystal,
        orient.reshape(512, 128),
        weight.reshape(GRAINS, 4096),
        cell_map.reshape(32, 128),
        density.transpose(0, 2, 1).reshape(128, 16),
        velocity.transpose(0, 1, 3, 2).reshape(384, 16),
        stress.transpose(0, 1, 3, 2).reshape(768, 16),
    )
    scratch = [
        (pltpu.SMEM if i == 1 else pltpu.VMEM)(array.shape, array.dtype)
        for i, array in enumerate(operands)
    ]
    scratch += [
        pltpu.VMEM((48, 128), F32),
        pltpu.VMEM((48, 128), I32),
        pltpu.VMEM((PARTS, 8, 128), F32),
        pltpu.VMEM((21, 8, 128), F32),
        pltpu.VMEM((512, 128), I32),
        pltpu.VMEM((32, 128), I32),
        pltpu.VMEM((32, 128), I32),
        pltpu.VMEM((16, ROWS, 128), F32),
        pltpu.VMEM((256, 128), F32),
        pltpu.VMEM((16, ROWS, 128), F32),
        pltpu.VMEM((16, ROWS, 128), F32),
        pltpu.VMEM((16, ROWS, 128), F32),
        pltpu.VMEM((8, 2, ROWS, 128), F32),
        pltpu.VMEM((8, 2, ROWS, 128), F32),
        pltpu.VMEM((21, 16, 128), F32),
    ]
    for count in (8, 2, 2, 15, 15, 7, 7):
        scratch.append(pltpu.SemaphoreType.DMA((count,)))
    steps = 2 * STEPS
    scratch += [
        pltpu.VMEM((steps, 3, 16, 128), F32),
        pltpu.VMEM((steps, 3, 8, 128), F32),
        pltpu.VMEM((steps, 3, 8, 128), F32),
        pltpu.VMEM((3, 32, 128), F32),
        pltpu.VMEM((steps, 2, 16, 128), F32),
        pltpu.VMEM((steps, 2, 16, 128), F32),
        pltpu.VMEM((steps, 3, 16, 128), F32),
        pltpu.VMEM((steps, 3, 16, 128), F32),
        pltpu.SemaphoreType.DMA((steps, 5)),
        pltpu.SemaphoreType.DMA((steps, 5)),
    ]
    stiffness, velocity, stress = pl.pallas_call(
        main_kernel,
        out_shape=(
            jax.ShapeDtypeStruct((2048, 21), F32),
            jax.ShapeDtypeStruct((384, 16), F32),
            jax.ShapeDtypeStruct((768, 16), F32),
        ),
        in_specs=[anywhere] * 8,
        out_specs=(vmem, vmem, vmem),
        scratch_shapes=scratch,
        compiler_params=pltpu.CompilerParams(
            collective_id=0, has_side_effects=True, vmem_limit_bytes=56 * 1024 * 1024
        ),
        name="relay_and_steps",
    )(*operands)
    return (
        stiffness.reshape(16, 16, 8, 21).transpose(3, 0, 1, 2),
        velocity.reshape(3, 16, 8, 16).transpose(0, 1, 3, 2),
        stress.reshape(6, 16, 8, 16).transpose(0, 1, 3, 2),
    )


def solution(mesh):
    fields = P(None, "gx", "gy", "ga")
    return jax.shard_map(
        on_device,
        mesh=mesh,
        in_specs=(
            P(),
            P(),
            P("ga", "gx", "gy", None),
            P("ga", "gx", "gy", None),
            P("gx", "gy", None),
            P("gx", "gy", "ga"),
            fields,
            fields,
        ),
        out_specs=(fields, fields, fields),
        check_vma=False,
    )
```

```python
import jax
import jax.numpy as jnp
import numpy as np
from jax import lax
from jax.experimental import pallas as pl
from jax.experimental.pallas import tpu as pltpu
from jax.sharding import PartitionSpec as P

MESH = pl.DeviceIdType.MESH
STEPS = 2
weights = (0.8, -0.2, 4.0 / 105.0, -1.0 / 280.0)
time_step = 0.2
voigt_pairs = ((0, 0), (1, 1), (2, 2), (1, 2), (0, 2), (0, 1))
upper_pairs = [(row, col) for row in range(6) for col in range(row, 6)]
F32, I32 = jnp.float32, jnp.int32
STRESS_X, STRESS_Y, STRESS_Z = (0, 5, 4), (5, 1, 3), (4, 3, 2)
GX, GY, GA = 16, 8, 2
GRAINS = 16
PARTS = 19
ROWS = 24
FULL = 32767.0
VMEM_LIMIT = 56 * 1024 * 1024
NEAR = 4


def upper(first, second):
    return upper_pairs.index((min(first, second), max(first, second)))


def ordered_sum(terms):
    total = terms[0]
    for term in terms[1:]:
        total = total + term
    return total


def entry_map(rotation):
    bond = np.zeros((6, 6))
    for i, (p, q) in enumerate(voigt_pairs):
        for j, (k, l) in enumerate(voigt_pairs):
            bond[i, j] = rotation[p, k] * rotation[q, l]
            if k != l:
                bond[i, j] += rotation[p, l] * rotation[q, k]
    image = np.zeros((21, 21))
    for n, (row, col) in enumerate(upper_pairs):
        unit = np.zeros((6, 6))
        unit[row, col] = unit[col, row] = 1.0
        turned = bond @ unit @ bond.T
        image[:, n] = [turned[i, j] for i, j in upper_pairs]
    return image


def turn(axis, angle):
    i, j = (axis + 1) % 3, (axis + 2) % 3
    out = np.eye(3)
    out[i, i] = out[j, j] = np.cos(angle)
    out[j, i] = np.sin(angle)
    out[i, j] = -out[j, i]
    return out


def harmonic_parts():
    size = np.sqrt([(1.0 + (r > 2)) * (1 + (c > 2)) * (1 + (r != c)) for r, c in upper_pairs])
    spins = []
    for axis in range(3):
        spin = np.zeros((21, 21))
        for n in range(16):
            angle = 2 * np.pi * n / 16
            image = size[:, None] * entry_map(turn(axis, angle)) / size
            spin += sum(m * np.sin(m * angle) for m in range(1, 5)) / 8 * image
        spins.append(spin)
    unit = np.eye(21)
    square = -(spins[0] @ spins[0] + spins[1] @ spins[1] + spins[2] @ spins[2])
    level = spins[2] @ spins[2]
    flat = unit
    for m in range(1, 5):
        flat = flat @ (unit + level / m**2)
    chosen = {0: (0, 1), 2: (upper(2, 2), upper(0, 1)), 4: (upper(2, 2),)}
    parts = []
    for degree, seeds in chosen.items():
        keep = flat
        for other in (0, 2, 4):
            if other != degree:
                first, last = degree * (degree + 1), other * (other + 1)
                keep = keep @ (square - last * unit) / (first - last)
        heads = []
        for seed in seeds:
            head = keep[:, seed]
            for former in heads:
                head = head - former * (former @ head)
            heads.append(head / np.linalg.norm(head))
            chain = [heads[-1]]
            for m in range(degree):
                step = spins[1] @ chain[m]
                if m:
                    step = step - chain[m - 1] * (chain[m - 1] @ step)
                chain.append(step / np.linalg.norm(step))
            part = [chain[0]]
            for m in range(1, degree + 1):
                part += [chain[m], spins[2] @ chain[m] / m]
            parts.append(np.stack(part, axis=1))
    basis = np.concatenate(parts[2:], axis=1)
    even = np.concatenate(parts[:2], axis=1)
    quarter = basis.T @ (size[:, None] * entry_map(turn(1, np.pi / 2)) / size) @ basis
    tables = (basis.T * size, basis / size[:, None], (even @ even.T) / size[:, None] * size, quarter)
    return [np.round(table, 9) for table in tables]


TO_PARTS, FROM_PARTS, EVEN, QUARTER = harmonic_parts()
BLOCKS = ((0, 2), (5, 2), (10, 4))


def sparse(row, values):
    terms = []
    for k in range(len(values)):
        factor = float(row[k])
        if factor:
            terms.append(values[k] if factor == 1 else -values[k] if factor == -1 else factor * values[k])
    return ordered_sum(terms) if terms else None


def quarter_turn(parts, matrix):
    out = []
    for start, degree in BLOCKS:
        stop = start + 2 * degree + 1
        out += [sparse(matrix[i, start:stop], parts[start:stop]) for i in range(start, stop)]
    return out


def about_z(parts, cos, sin):
    out = []
    for start, degree in BLOCKS:
        out.append(parts[start] if cos[0] is None else parts[start] * cos[0])
        for m in range(1, degree + 1):
            a, b = parts[start + 2 * m - 1], parts[start + 2 * m]
            out += [a * cos[m] - b * sin[m], a * sin[m] + b * cos[m]]
    return out


def multiples(cos, sin):
    twice = cos + cos
    cos, sin = [None, cos, twice * cos - 1.0], [None, sin, twice * sin]
    for m in (3, 4):
        cos.append(twice * cos[m - 1] - cos[m - 2])
        sin.append(twice * sin[m - 1] - sin[m - 2])
    return cos, sin


def lane_pick(row, index):
    return jnp.take_along_axis(row, index, axis=1, mode="promise_in_bounds")


def sublane_pick(block, index):
    return jnp.take_along_axis(block, index, axis=0, mode="promise_in_bounds")


def tree(values, masks):
    for mask in masks:
        values = [
            jnp.where(mask, values[2 * i + 1], values[2 * i]) for i in range(len(values) // 2)
        ]
    return values[0]


def lane_iota(rows):
    return lax.broadcasted_iota(I32, (rows, 128), 1)


def row_iota(rows):
    return lax.broadcasted_iota(I32, (rows, 128), 0)


def pair_word(first, second):
    low = jnp.floor(second * FULL + 0.5)
    high = jnp.floor(first * FULL - low * (1.0 / 65536.0) + 0.5).astype(I32)
    return high * 65536 + low.astype(I32)


def prepare_table(euler, crystal, angles, table, seeds, even):
    for j in range(16):
        angles[pl.ds(j, 3, stride=16), :] = euler[:, j * 128 : (j + 1) * 128]
    for k in range(3):
        angle = angles[k * 16 : k * 16 + 16, :]
        table[k * 16 : k * 16 + 16, :] = pair_word(jnp.cos(angle), jnp.sin(angle))
    values = [jnp.full((8, 128), crystal[i], F32) for i in range(21)]
    for i in range(PARTS):
        seeds[i] = sparse(TO_PARTS[i], values)
    for i in range(21):
        found = sparse(EVEN[i], values)
        even[i] = jnp.zeros((8, 128), F32) if found is None else found


def prepare_cells(orient, weight, cell_map, packed, from_row, from_lane):
    for j in range(32):
        mass = (weight[:, j * 128 : (j + 1) * 128].astype(F32) * 2048.0).astype(I32)
        chosen = orient[pl.ds(j, GRAINS, stride=32), :]
        packed[pl.ds(j, GRAINS, stride=32), :] = chosen * 4096 + mass
    me_x, me_a = lax.axis_index("gx"), lax.axis_index("ga")
    slot = cell_map[...]
    depth = slot & 15
    own = ((depth >> 3) == me_a).astype(I32)
    to_row = own * 16 + (((slot >> 8) - me_x + (GX - NEAR)) & 15)
    to_lane = ((slot >> 4) & 15) * 8 + (depth & 7)
    rows, lanes = row_iota(32), row_iota(128)
    here = lane_iota(32).astype(F32)
    found = jnp.zeros((64, 128), F32)
    for j in range(32):
        hit = rows == jnp.broadcast_to(to_row[j : j + 1, :], (32, 128))
        left = jnp.concatenate(
            [jnp.where(hit, float(j), 0.0), jnp.where(hit, here, 0.0)], axis=0
        ).astype(jnp.bfloat16)
        right = jnp.where(lanes == jnp.broadcast_to(to_lane[j : j + 1, :], (128, 128)), 1.0, 0.0)
        found = found + lax.dot_general(
            left,
            right.astype(jnp.bfloat16),
            (((1,), (1,)), ((), ())),
            preferred_element_type=F32,
        )
    found = (found + 0.5).astype(I32)
    from_row[...] = found[:32]
    from_lane[...] = found[32:]


def grain_sums(table, seeds, packed, from_row, from_lane, start):
    lane = from_lane[start : start + 8, :]
    row = from_row[start : start + 8, :]
    row_bits = [((row >> bit) & 1) == 1 for bit in range(5)]

    def fetch(grain):
        return tree(
            [
                lane_pick(jnp.broadcast_to(packed[pl.ds(grain * 32 + j, 1), :], (8, 128)), lane)
                for j in range(32)
            ],
            row_bits,
        )

    def angles_of(word):
        spot = (word >> 12) & 127
        bits = [((word >> (19 + bit)) & 1) == 1 for bit in range(4)]
        return [
            tree(
                [
                    lane_pick(
                        jnp.broadcast_to(table[k * 16 + h : k * 16 + h + 1, :], (8, 128)), spot
                    )
                    for h in range(16)
                ],
                bits,
            )
            for k in range(3)
        ]

    def absorb(grain, carry):
        word, pairs, sums = carry[0], carry[1:4], carry[4:]
        coming = carry[0 + 4 + PARTS + 1]
        sums = sums[: PARTS + 1]
        after = fetch(jnp.minimum(grain + 2, GRAINS - 1))
        coming_pairs = angles_of(coming)
        mass = (word & 4095).astype(F32)
        unit = 1.0 / (FULL * 65536.0)
        turns = [
            multiples(pair.astype(F32) * unit, (pair << 16).astype(F32) * unit) for pair in pairs
        ]
        cos, sin = turns[2]
        cos = [mass] + [mass * value for value in cos[1:]]
        sin = [None] + [mass * value for value in sin[1:]]
        parts = about_z([seeds[i] for i in range(PARTS)], cos, sin)
        parts = quarter_turn(parts, QUARTER.T)
        parts = about_z(parts, *turns[1])
        parts = quarter_turn(parts, QUARTER)
        parts = about_z(parts, *turns[0])
        out = [old + new for old, new in zip(sums, parts)] + [sums[PARTS] + mass]
        return (coming, *coming_pairs, *out, after)

    zero = jnp.zeros((8, 128), F32)
    first, second = fetch(0), fetch(1)
    carry = (first, *angles_of(first)) + (zero,) * (PARTS + 1) + (second,)
    return lax.fori_loop(0, GRAINS, absorb, carry)[4 : 4 + PARTS + 1]


def block_swap(block, regroup):
    sublane, lane = row_iota(8), lane_iota(8)
    group, place = lane >> 4, lane & 15
    skewed = lane_pick(block, ((group + sublane) & 7) * 16 + place)
    skewed = sublane_pick(skewed, (sublane - group) & 7)
    if regroup:
        y, z = lane & 15, lane >> 4
        group, place = y >> 1, (y & 1) * 8 + z
    return lane_pick(skewed, ((sublane - group) & 7) * 16 + place)


def along_y(field, k, low, high):
    y = lane_iota(16) & 15
    low = pltpu.roll(low, 128 - (4 + 4 * k), 1)
    high = pltpu.roll(high, 16 - 4 * k, 1)
    total = None
    for m in range(1, 5):
        up = pltpu.roll(jnp.where(y < m, high, field), 128 - m, 1)
        down = pltpu.roll(jnp.where(y >= 16 - m, low, field), m, 1)
        term = weights[m - 1] * (up - down)
        total = term if total is None else total + term
    return total


def along_z(field, low, high):
    z = lane_iota(16) >> 4
    total = None
    for m in range(1, 5):
        up = pltpu.roll(jnp.where(z < m, high, field), 128 - 16 * m, 1)
        down = pltpu.roll(jnp.where(z >= 8 - m, low, field), 16 * m, 1)
        term = weights[m - 1] * (up - down)
        total = term if total is None else total + term
    return total


def along_x(padded):
    total = None
    for m in range(1, 5):
        term = weights[m - 1] * (padded[8 + m : 24 + m, :] - padded[8 - m : 24 - m, :])
        total = term if total is None else total + term
    return total


class Halo:
    def __init__(self, step, refs, me):
        self.step, self.me = step, me
        self.xs, self.xl, self.xr, self.xb, self.ys, self.yr, self.zs, self.zr, send, recv = refs
        x, y, a = me
        ends = [((x + 1) % GX, y, a), ((x + GX - 1) % GX, y, a)]
        ends += [(x, (y + 1) % GY, a), (x, (y + GY - 1) % GY, a), (x, y, 1 - a)]
        i = step
        pairs = [
            (self.xs.at[i, :, 8:16], self.xl.at[i]),
            (self.xs.at[i, :, 0:8], self.xr.at[i]),
            (self.ys.at[i, 0], self.yr.at[i, 0]),
            (self.ys.at[i, 1], self.yr.at[i, 1]),
            (self.zs.at[i], self.zr.at[i]),
        ]
        self.copies = [
            pltpu.make_async_remote_copy(
                src_ref=source,
                dst_ref=target,
                send_sem=send.at[i, n],
                recv_sem=recv.at[i, n],
                device_id=end,
                device_id_type=MESH,
            )
            for n, ((source, target), end) in enumerate(zip(pairs, ends))
        ]

    def start(self, along):
        self.fields = along
        fx, fy, fz = along
        i = self.step
        quarter = (lane_iota(16) & 15) >> 2
        for k in range(3):
            self.xs[i, k] = fx[k]
        self.copies[0].start()
        self.copies[1].start()
        for side, offset in ((0, 128 - 12), (1, 0)):
            rolled = [
                pltpu.roll(fy[k], (offset + 4 * k) % 128, 1) if (offset + 4 * k) % 128 else fy[k]
                for k in range(3)
            ]
            self.ys[i, side] = jnp.where(
                quarter == 0, rolled[0], jnp.where(quarter == 1, rolled[1], rolled[2])
            )
            self.copies[2 + side].start()
        for k in range(3):
            self.zs[i, k] = fz[k]
        self.copies[4].start()

    def finish(self):
        x, y, a = self.me
        fx, fy, fz = self.fields
        i = self.step
        for copy in self.copies:
            copy.wait()
        for k in range(3):
            self.xb[k, 0:8, :] = jnp.where(x > 0, self.xl[i, k], 0.0)
            self.xb[k, 8:24, :] = fx[k]
            self.xb[k, 24:32, :] = jnp.where(x < GX - 1, self.xr[i, k], 0.0)
        dx = [along_x(self.xb.at[k]) for k in range(3)]
        low = jnp.where(y > 0, self.yr[i, 0], 0.0)
        high = jnp.where(y < GY - 1, self.yr[i, 1], 0.0)
        dy = [along_y(fy[k], k, low, high) for k in range(3)]
        dz = []
        for k in range(3):
            other = self.zr[i, k]
            dz.append(
                along_z(fz[k], jnp.where(a > 0, other, 0.0), jnp.where(a == 0, other, 0.0))
            )
        return dx, dy, dz


def new_velocity(velocity, diffs, factor):
    dx, dy, dz = diffs
    return [velocity[k] + (dx[k] + dy[k] + dz[k]) * factor for k in range(3)]


def strain_rates(diffs):
    dx, dy, dz = diffs
    return [dx[0], dy[1], dz[2], dy[2] + dz[1], dx[2] + dz[0], dx[1] + dy[0]]


def new_stress(stress, strain, stiffness):
    return [
        stress[row]
        + time_step
        * ordered_sum([stiffness[upper(row, col)] * strain[col] for col in range(6)])
        for row in range(6)
    ]


def stress_parts(stress):
    return tuple([stress[i] for i in which] for which in (STRESS_X, STRESS_Y, STRESS_Z))


def entries_of(parts, even):
    out = []
    for i in range(21):
        entry = sparse(FROM_PARTS[i], parts)
        if EVEN[i].any():
            constant = jnp.concatenate([even[i], even[i]], axis=0)
            entry = constant if entry is None else entry + constant
        out.append(entry)
    return out


def main_kernel(*refs):
    given, outs, refs = refs[:8], refs[8:10], refs[10:]
    held, refs = refs[:8], refs[8:]
    angles, table, seeds, even, packed, from_row, from_lane, partial = refs[:8]
    refs = refs[8:]
    fields, arrived, first, first_in, second, second_in, stiff, waves = refs[:8]
    load_sem, out_sem = refs[8:10]
    rs_send, rs_recv, p1_send, p1_recv, p2_send, p2_recv = refs[10:16]
    halo_refs = refs[16:]
    stores = [
        pltpu.make_async_copy(stiff, outs[0], out_sem.at[0]),
        pltpu.make_async_copy(waves.at[0:48], outs[1].at[0:48], out_sem.at[1]),
        pltpu.make_async_copy(waves.at[48:144], outs[1].at[48:144], out_sem.at[2]),
    ]

    loads = [pltpu.make_async_copy(given[i], held[i], load_sem.at[i]) for i in range(8)]
    for load in loads:
        load.start()
    euler, crystal, orient, weight, cell_map, density, velocity, stress = held
    x, y, a = lax.axis_index("gx"), lax.axis_index("gy"), lax.axis_index("ga")
    barrier = pltpu.get_barrier_semaphore()
    ends = [((x + d) % GX, y, a) for d in range(1, GX)]
    ends += [(x, (y + d) % GY, a) for d in range(1, GY)]
    ends += [(x, y, 1 - a)]
    for end in ends:
        pl.semaphore_signal(barrier, inc=1, device_id=end, device_id_type=MESH)

    loads[0].wait()
    loads[1].wait()
    prepare_table(euler, crystal, angles, table, seeds, even)
    for i in range(2, 5):
        loads[i].wait()
    prepare_cells(orient, weight, cell_map, packed, from_row, from_lane)

    halos = [Halo(step, halo_refs, (x, y, a)) for step in range(2 * STEPS)]
    half = [
        pltpu.make_async_remote_copy(
            src_ref=partial.at[pl.ds(i * 8, 8), 0 : PARTS + 1],
            dst_ref=arrived.at[pl.ds(i * 8, 8), 0 : PARTS + 1],
            send_sem=rs_send.at[i],
            recv_sem=rs_recv.at[i],
            device_id=(x, y, 1 - a),
            device_id_type=MESH,
        )
        for i in range(2)
    ]
    to_brick = {}
    for row in range(16):
        d = (row + NEAR) % GX
        if d:
            to_brick[row] = pltpu.make_async_remote_copy(
                src_ref=first.at[row, 0:PARTS],
                dst_ref=first_in.at[x, 0:PARTS],
                send_sem=p1_send.at[d - 1],
                recv_sem=p1_recv.at[d - 1],
                device_id=((x + d) % GX, y, a),
                device_id_type=MESH,
            )

    def sums_of(start):
        return grain_sums(table, seeds, packed, from_row, from_lane, start)

    def other_half(i):
        sums = sums_of(i * 8)
        for c in range(PARTS + 1):
            partial[i * 8 : i * 8 + 8, c, :] = sums[c]

    def own_half(i):
        sums = sums_of(16 + i * 8)
        half[i].wait()
        rows = slice(i * 8, i * 8 + 8)
        gain = 1.0 / (sums[PARTS] + arrived[rows, PARTS, :])
        for c in range(PARTS):
            first[rows, c, :] = (sums[c] + arrived[rows, c, :]) * gain
        for row in range(i * 8, i * 8 + 8):
            if row in to_brick:
                to_brick[row].start()

    other_half(0)
    for i in range(5, 8):
        loads[i].wait()
    for z in range(8):
        lanes = slice(z * 16, z * 16 + 16)
        fields[0:96, lanes] = stress[pl.ds(z, 96, stride=8), :]
        fields[96:144, lanes] = velocity[pl.ds(z, 48, stride=8), :]
        fields[144:160, lanes] = density[pl.ds(z, 16, stride=8), :]
    stresses = [fields[i * 16 : i * 16 + 16, :] for i in range(6)]
    pl.semaphore_wait(barrier, len(ends))
    half[0].start()
    halos[0].start(stress_parts(stresses))
    other_half(1)
    half[1].start()
    own_half(0)
    factor = time_step / fields[144:160, :]
    velocities = [fields[96 + k * 16 : 112 + k * 16, :] for k in range(3)]
    velocities = new_velocity(velocities, halos[0].finish(), factor)
    for k in range(3):
        fields[96 + k * 16 : 112 + k * 16, :] = velocities[k]
    fields[144:160, :] = factor
    halos[1].start((velocities,) * 3)
    own_half(1)
    velocities = [fields[96 + k * 16 : 112 + k * 16, :] for k in range(3)]
    halos[1].fields = (velocities,) * 3
    strain = strain_rates(halos[1].finish())
    for i in range(6):
        fields[160 + i * 16 : 176 + i * 16, :] = strain[i]
    first_in[x, 0:PARTS, :] = first[GX - NEAR, 0:PARTS, :]
    for copy in to_brick.values():
        copy.wait()

    for p in range(2):
        for c in range(PARTS):
            block = first_in[p * 8 : p * 8 + 8, c, :]
            second[:, p, c, :] = block_swap(block, False)
    to_y = []
    for d in range(1, GY):
        target = (y + d) % GY
        copy = pltpu.make_async_remote_copy(
            src_ref=second.at[target, :, 0:PARTS],
            dst_ref=second_in.at[y, :, 0:PARTS],
            send_sem=p2_send.at[d - 1],
            recv_sem=p2_recv.at[d - 1],
            device_id=(x, target, a),
            device_id_type=MESH,
        )
        copy.start()
        to_y.append(copy)
    for p in range(2):
        second_in[y, p, 0:PARTS, :] = second[y, p, 0:PARTS, :]
    for copy in to_y:
        copy.wait()
    parts = []
    for c in range(PARTS):
        parts.append(
            jnp.concatenate([block_swap(second_in[:, p, c, :], True) for p in range(2)], axis=0)
        )
    for i, entry in enumerate(entries_of(parts, even)):
        stiff[i] = entry

    strain = [fields[160 + i * 16 : 176 + i * 16, :] for i in range(6)]
    stresses = [fields[i * 16 : i * 16 + 16, :] for i in range(6)]
    stresses = new_stress(stresses, strain, stiff)
    halos[2].start(stress_parts(stresses))
    stores[0].start()
    factor = fields[144:160, :]
    velocities = [fields[96 + k * 16 : 112 + k * 16, :] for k in range(3)]
    velocities = new_velocity(velocities, halos[2].finish(), factor)
    halos[3].start((velocities,) * 3)
    for k in range(3):
        waves[k * 16 : k * 16 + 16, :] = velocities[k]
    stores[1].start()
    strain = strain_rates(halos[3].finish())
    stresses = new_stress(stresses, strain, stiff)
    for k in range(6):
        waves[48 + k * 16 : 64 + k * 16, :] = stresses[k]
    stores[2].start()
    for store in stores:
        store.wait()


def layout_kernel(
    stiff_in, waves_in, stiff_out, velocity_out, stress_out,
    stiff, waves, stiff_held, velocity_held, stress_held, sems, load_sems,
):
    loads = [
        pltpu.make_async_copy(waves_in, waves, load_sems.at[0]),
        pltpu.make_async_copy(stiff_in, stiff, load_sems.at[1]),
    ]
    for load in loads:
        load.start()
    loads[0].wait()
    copies = []

    def send(source, target):
        copies.append(pltpu.make_async_copy(source, target, sems.at[len(copies)]))
        copies[-1].start()

    for z in range(8):
        lanes = slice(z * 16, z * 16 + 16)
        stress_held[pl.ds(z, 96, stride=8), :] = waves[48:144, lanes]
        velocity_held[pl.ds(z, 48, stride=8), :] = waves[0:48, lanes]
    send(stress_held, stress_out)
    send(velocity_held, velocity_out)
    loads[1].wait()
    for row in range(16):
        turned = jnp.transpose(stiff[:, row, :], (1, 0))
        for z in range(8):
            stiff_held[pl.ds(row * 128 + z, 16, stride=8), :] = turned[z * 16 : z * 16 + 16, :21]
        if row % 4 == 3:
            rows = pl.ds((row - 3) * 128, 512)
            send(stiff_held.at[rows, :], stiff_out.at[rows, :])
    for copy in copies:
        copy.wait()


def on_device(euler_table, crystal, orient, weight, cell_map, density, velocity, stress):
    anywhere = pl.BlockSpec(memory_space=pl.ANY)
    operands = (
        euler_table,
        crystal,
        orient.reshape(512, 128),
        weight.reshape(GRAINS, 4096),
        cell_map.reshape(32, 128),
        density.transpose(0, 2, 1).reshape(128, 16),
        velocity.transpose(0, 1, 3, 2).reshape(384, 16),
        stress.transpose(0, 1, 3, 2).reshape(768, 16),
    )
    scratch = [
        (pltpu.SMEM if i == 1 else pltpu.VMEM)(array.shape, array.dtype)
        for i, array in enumerate(operands)
    ]
    scratch += [
        pltpu.VMEM((48, 128), F32),
        pltpu.VMEM((48, 128), I32),
        pltpu.VMEM((PARTS, 8, 128), F32),
        pltpu.VMEM((21, 8, 128), F32),
        pltpu.VMEM((512, 128), I32),
        pltpu.VMEM((32, 128), I32),
        pltpu.VMEM((32, 128), I32),
        pltpu.VMEM((16, ROWS, 128), F32),
        pltpu.VMEM((256, 128), F32),
        pltpu.VMEM((16, ROWS, 128), F32),
        pltpu.VMEM((16, ROWS, 128), F32),
        pltpu.VMEM((16, ROWS, 128), F32),
        pltpu.VMEM((8, 2, ROWS, 128), F32),
        pltpu.VMEM((8, 2, ROWS, 128), F32),
    ]
    small = (jax.ShapeDtypeStruct((21, 16, 128), F32), jax.ShapeDtypeStruct((144, 128), F32))
    small_held = [pltpu.VMEM(array.shape, F32) for array in small]
    scratch += small_held
    for count in (8, 3, 2, 2, 15, 15, 7, 7):
        scratch.append(pltpu.SemaphoreType.DMA((count,)))
    steps = 2 * STEPS
    scratch += [
        pltpu.VMEM((steps, 3, 16, 128), F32),
        pltpu.VMEM((steps, 3, 8, 128), F32),
        pltpu.VMEM((steps, 3, 8, 128), F32),
        pltpu.VMEM((3, 32, 128), F32),
        pltpu.VMEM((steps, 2, 16, 128), F32),
        pltpu.VMEM((steps, 2, 16, 128), F32),
        pltpu.VMEM((steps, 3, 16, 128), F32),
        pltpu.VMEM((steps, 3, 16, 128), F32),
        pltpu.SemaphoreType.DMA((steps, 5)),
        pltpu.SemaphoreType.DMA((steps, 5)),
    ]
    found = pl.pallas_call(
        main_kernel,
        out_shape=small,
        in_specs=[anywhere] * 8,
        out_specs=(anywhere, anywhere),
        scratch_shapes=scratch,
        compiler_params=pltpu.CompilerParams(
            collective_id=0, has_side_effects=True, vmem_limit_bytes=VMEM_LIMIT
        ),
        name="relay_and_steps",
    )(*operands)
    shapes = ((2048, 21), (384, 16), (768, 16))
    stiffness, velocity, stress = pl.pallas_call(
        layout_kernel,
        out_shape=tuple(jax.ShapeDtypeStruct(shape, F32) for shape in shapes),
        in_specs=[anywhere, anywhere],
        out_specs=(anywhere,) * 3,
        scratch_shapes=small_held
        + [pltpu.VMEM(shape, F32) for shape in shapes]
        + [pltpu.SemaphoreType.DMA((6,)), pltpu.SemaphoreType.DMA((2,))],
        compiler_params=pltpu.CompilerParams(vmem_limit_bytes=VMEM_LIMIT),
        name="layouts",
    )(*found)
    return (
        stiffness.reshape(16, 16, 8, 21).transpose(3, 0, 1, 2),
        velocity.reshape(3, 16, 8, 16).transpose(0, 1, 3, 2),
        stress.reshape(6, 16, 8, 16).transpose(0, 1, 3, 2),
    )


def solution(mesh):
    fields = P(None, "gx", "gy", "ga")
    return jax.shard_map(
        on_device,
        mesh=mesh,
        in_specs=(
            P(),
            P(),
            P("ga", "gx", "gy", None),
            P("ga", "gx", "gy", None),
            P("gx", "gy", None),
            P("gx", "gy", "ga"),
            fields,
            fields,
        ),
        out_specs=(fields, fields, fields),
        check_vma=False,
    )
```

```python
import jax
import jax.numpy as jnp
import numpy as np
from jax import lax
from jax.experimental import pallas as pl
from jax.experimental.pallas import tpu as pltpu
from jax.sharding import PartitionSpec as P

MESH = pl.DeviceIdType.MESH
STEPS = 2
weights = (0.8, -0.2, 4.0 / 105.0, -1.0 / 280.0)
time_step = 0.2
voigt_pairs = ((0, 0), (1, 1), (2, 2), (1, 2), (0, 2), (0, 1))
upper_pairs = [(row, col) for row in range(6) for col in range(row, 6)]
F32, I32 = jnp.float32, jnp.int32
STRESS_X, STRESS_Y, STRESS_Z = (0, 5, 4), (5, 1, 3), (4, 3, 2)
GX, GY, GA = 16, 8, 2
GRAINS = 16
PARTS = 19
ROWS = 24
STEP = 1 << 19
VMEM_LIMIT = 56 * 1024 * 1024
NEAR = 4


def upper(first, second):
    return upper_pairs.index((min(first, second), max(first, second)))


def ordered_sum(terms):
    total = terms[0]
    for term in terms[1:]:
        total = total + term
    return total


def entry_map(rotation):
    bond = np.zeros((6, 6))
    for i, (p, q) in enumerate(voigt_pairs):
        for j, (k, l) in enumerate(voigt_pairs):
            bond[i, j] = rotation[p, k] * rotation[q, l]
            if k != l:
                bond[i, j] += rotation[p, l] * rotation[q, k]
    image = np.zeros((21, 21))
    for n, (row, col) in enumerate(upper_pairs):
        unit = np.zeros((6, 6))
        unit[row, col] = unit[col, row] = 1.0
        turned = bond @ unit @ bond.T
        image[:, n] = [turned[i, j] for i, j in upper_pairs]
    return image


def turn(axis, angle):
    i, j = (axis + 1) % 3, (axis + 2) % 3
    out = np.eye(3)
    out[i, i] = out[j, j] = np.cos(angle)
    out[j, i] = np.sin(angle)
    out[i, j] = -out[j, i]
    return out


def harmonic_parts():
    size = np.sqrt([(1.0 + (r > 2)) * (1 + (c > 2)) * (1 + (r != c)) for r, c in upper_pairs])
    spins = []
    for axis in range(3):
        spin = np.zeros((21, 21))
        for n in range(16):
            angle = 2 * np.pi * n / 16
            image = size[:, None] * entry_map(turn(axis, angle)) / size
            spin += sum(m * np.sin(m * angle) for m in range(1, 5)) / 8 * image
        spins.append(spin)
    unit = np.eye(21)
    square = -(spins[0] @ spins[0] + spins[1] @ spins[1] + spins[2] @ spins[2])
    level = spins[2] @ spins[2]
    flat = unit
    for m in range(1, 5):
        flat = flat @ (unit + level / m**2)
    chosen = {0: (0, 1), 2: (upper(2, 2), upper(0, 1)), 4: (upper(2, 2),)}
    parts = []
    for degree, seeds in chosen.items():
        keep = flat
        for other in (0, 2, 4):
            if other != degree:
                first, last = degree * (degree + 1), other * (other + 1)
                keep = keep @ (square - last * unit) / (first - last)
        heads = []
        for seed in seeds:
            head = keep[:, seed]
            for former in heads:
                head = head - former * (former @ head)
            heads.append(head / np.linalg.norm(head))
            chain = [heads[-1]]
            for m in range(degree):
                step = spins[1] @ chain[m]
                if m:
                    step = step - chain[m - 1] * (chain[m - 1] @ step)
                chain.append(step / np.linalg.norm(step))
            part = [chain[0]]
            for m in range(1, degree + 1):
                part += [chain[m], spins[2] @ chain[m] / m]
            parts.append(np.stack(part, axis=1))
    basis = np.concatenate(parts[2:], axis=1)
    even = np.concatenate(parts[:2], axis=1)
    quarter = basis.T @ (size[:, None] * entry_map(turn(1, np.pi / 2)) / size) @ basis
    tables = (basis.T * size, basis / size[:, None], (even @ even.T) / size[:, None] * size, quarter)
    return [np.round(table, 9) for table in tables]


TO_PARTS, FROM_PARTS, EVEN, QUARTER = harmonic_parts()
BLOCKS = ((0, 2), (5, 2), (10, 4))


def sparse(row, values):
    terms = []
    for k in range(len(values)):
        factor = float(row[k])
        if factor:
            terms.append(values[k] if factor == 1 else -values[k] if factor == -1 else factor * values[k])
    return ordered_sum(terms) if terms else None


def quarter_turn(parts, matrix):
    out = []
    for start, degree in BLOCKS:
        stop = start + 2 * degree + 1
        out += [sparse(matrix[i, start:stop], parts[start:stop]) for i in range(start, stop)]
    return out


def about_z(parts, cos, sin):
    out = []
    for start, degree in BLOCKS:
        out.append(parts[start] if cos[0] is None else parts[start] * cos[0])
        for m in range(1, degree + 1):
            a, b = parts[start + 2 * m - 1], parts[start + 2 * m]
            out += [a * cos[m] - b * sin[m], a * sin[m] + b * cos[m]]
    return out


def multiples(cos, sin):
    twice = cos + cos
    cos, sin = [None, cos, twice * cos - 1.0], [None, sin, twice * sin]
    for m in (3, 4):
        cos.append(twice * cos[m - 1] - cos[m - 2])
        sin.append(twice * sin[m - 1] - sin[m - 2])
    return cos, sin


def lane_pick(row, index):
    return jnp.take_along_axis(row, index, axis=1, mode="promise_in_bounds")


def sublane_pick(block, index):
    return jnp.take_along_axis(block, index, axis=0, mode="promise_in_bounds")


def tree(values, masks):
    for mask in masks:
        values = [
            jnp.where(mask, values[2 * i + 1], values[2 * i]) for i in range(len(values) // 2)
        ]
    return values[0]


def lane_iota(rows):
    return lax.broadcasted_iota(I32, (rows, 128), 1)


def row_iota(rows):
    return lax.broadcasted_iota(I32, (rows, 128), 0)


def angle_field(angle):
    cos, sin = jnp.cos(angle), jnp.sin(angle)
    back = cos < 0.0
    tangent = jnp.where(back, -sin, sin) / (1.0 + jnp.abs(cos))
    whole = jnp.floor(tangent * STEP + 0.5).astype(I32)
    return jnp.clip(whole, -STEP, STEP - 1) * 2 + back.astype(I32)


def cos_sin(field):
    tangent = field.astype(F32) * (0.5 / STEP)
    square = tangent * tangent
    below = 1.0 + square
    rough = pl.reciprocal(below, approx=True)
    fine = rough * (2.0 - below * rough)
    fine = jnp.where((field & 1) == 1, -fine, fine)
    return (1.0 - square) * fine, (tangent + tangent) * fine


def prepare_table(euler, crystal, angles, table, seeds, even):
    for j in range(16):
        angles[pl.ds(j, 3, stride=16), :] = euler[:, j * 128 : (j + 1) * 128]
    turns = [angle_field(angles[k * 16 : k * 16 + 16, :]) for k in range(3)]
    last = turns[2] + 2 * STEP
    table[0:16, :] = turns[0] * 2048 + (last >> 11)
    table[16:32, :] = turns[1] * 2048 + (last & 2047)
    values = [jnp.full((8, 128), crystal[i], F32) for i in range(21)]
    for i in range(PARTS):
        seeds[i] = sparse(TO_PARTS[i], values)
    for i in range(21):
        found = sparse(EVEN[i], values)
        even[i] = jnp.zeros((8, 128), F32) if found is None else found


def prepare_cells(orient, weight, cell_map, packed, from_row, from_lane):
    for j in range(32):
        mass = (weight[:, j * 128 : (j + 1) * 128].astype(F32) * 2048.0).astype(I32)
        chosen = orient[pl.ds(j, GRAINS, stride=32), :]
        packed[pl.ds(j, GRAINS, stride=32), :] = chosen * 4096 + mass
    me_x, me_a = lax.axis_index("gx"), lax.axis_index("ga")
    slot = cell_map[...]
    depth = slot & 15
    own = ((depth >> 3) == me_a).astype(I32)
    to_row = own * 16 + (((slot >> 8) - me_x + (GX - NEAR)) & 15)
    to_lane = ((slot >> 4) & 15) * 8 + (depth & 7)
    rows, lanes = row_iota(32), row_iota(128)
    here = lane_iota(32).astype(F32)
    found = jnp.zeros((64, 128), F32)
    for j in range(32):
        hit = rows == jnp.broadcast_to(to_row[j : j + 1, :], (32, 128))
        left = jnp.concatenate(
            [jnp.where(hit, float(j), 0.0), jnp.where(hit, here, 0.0)], axis=0
        ).astype(jnp.bfloat16)
        right = jnp.where(lanes == jnp.broadcast_to(to_lane[j : j + 1, :], (128, 128)), 1.0, 0.0)
        found = found + lax.dot_general(
            left,
            right.astype(jnp.bfloat16),
            (((1,), (1,)), ((), ())),
            preferred_element_type=F32,
        )
    found = (found + 0.5).astype(I32)
    from_row[...] = found[:32]
    from_lane[...] = found[32:]


def grain_sums(table, seeds, packed, from_row, from_lane, start):
    lane = from_lane[start : start + 8, :]
    row = from_row[start : start + 8, :]
    row_bits = [((row >> bit) & 1) == 1 for bit in range(5)]

    def fetch(grain):
        return tree(
            [
                lane_pick(jnp.broadcast_to(packed[pl.ds(grain * 32 + j, 1), :], (8, 128)), lane)
                for j in range(32)
            ],
            row_bits,
        )

    def angles_of(word):
        spot = (word >> 12) & 127
        bits = [((word >> (19 + bit)) & 1) == 1 for bit in range(4)]
        return [
            tree(
                [
                    lane_pick(
                        jnp.broadcast_to(table[k * 16 + h : k * 16 + h + 1, :], (8, 128)), spot
                    )
                    for h in range(16)
                ],
                bits,
            )
            for k in range(2)
        ]

    def absorb(grain, carry):
        word, coming, one, two = carry[:4]
        sums = carry[4:]
        after = fetch(jnp.minimum(grain + 2, GRAINS - 1))
        coming_pair = angles_of(coming)
        mass = (word & 4095).astype(F32)
        fields = (one >> 11, two >> 11, ((one & 1023) << 11) + (two & 2047) - 2 * STEP)
        turns = [multiples(*cos_sin(field)) for field in fields]
        cos, sin = turns[2]
        cos = [mass] + [mass * value for value in cos[1:]]
        sin = [None] + [mass * value for value in sin[1:]]
        parts = about_z([seeds[i] for i in range(PARTS)], cos, sin)
        parts = quarter_turn(parts, QUARTER.T)
        parts = about_z(parts, *turns[1])
        parts = quarter_turn(parts, QUARTER)
        parts = about_z(parts, *turns[0])
        out = [old + new for old, new in zip(sums, parts)] + [sums[PARTS] + mass]
        return (coming, after, *coming_pair, *out)

    zero = jnp.zeros((8, 128), F32)
    first, second = fetch(0), fetch(1)
    carry = (first, second, *angles_of(first)) + (zero,) * (PARTS + 1)
    return lax.fori_loop(0, GRAINS, absorb, carry)[4:]


def block_swap(block, regroup):
    sublane, lane = row_iota(8), lane_iota(8)
    group, place = lane >> 4, lane & 15
    skewed = lane_pick(block, ((group + sublane) & 7) * 16 + place)
    skewed = sublane_pick(skewed, (sublane - group) & 7)
    if regroup:
        y, z = lane & 15, lane >> 4
        group, place = y >> 1, (y & 1) * 8 + z
    return lane_pick(skewed, ((sublane - group) & 7) * 16 + place)


def along_y(field, k, low, high):
    y = lane_iota(16) & 15
    low = pltpu.roll(low, 128 - (4 + 4 * k), 1)
    high = pltpu.roll(high, 16 - 4 * k, 1)
    total = None
    for m in range(1, 5):
        up = pltpu.roll(jnp.where(y < m, high, field), 128 - m, 1)
        down = pltpu.roll(jnp.where(y >= 16 - m, low, field), m, 1)
        term = weights[m - 1] * (up - down)
        total = term if total is None else total + term
    return total


def along_z(field, low, high):
    z = lane_iota(16) >> 4
    total = None
    for m in range(1, 5):
        up = pltpu.roll(jnp.where(z < m, high, field), 128 - 16 * m, 1)
        down = pltpu.roll(jnp.where(z >= 8 - m, low, field), 16 * m, 1)
        term = weights[m - 1] * (up - down)
        total = term if total is None else total + term
    return total


def along_x(padded):
    total = None
    for m in range(1, 5):
        term = weights[m - 1] * (padded[8 + m : 24 + m, :] - padded[8 - m : 24 - m, :])
        total = term if total is None else total + term
    return total


class Halo:
    def __init__(self, step, refs, me):
        self.step, self.me = step, me
        self.xs, self.xl, self.xr, self.xb, self.ys, self.yr, self.zs, self.zr, send, recv = refs
        x, y, a = me
        ends = [((x + 1) % GX, y, a), ((x + GX - 1) % GX, y, a)]
        ends += [(x, (y + 1) % GY, a), (x, (y + GY - 1) % GY, a), (x, y, 1 - a)]
        i = step
        pairs = [
            (self.xs.at[i, :, 8:16], self.xl.at[i]),
            (self.xs.at[i, :, 0:8], self.xr.at[i]),
            (self.ys.at[i, 0], self.yr.at[i, 0]),
            (self.ys.at[i, 1], self.yr.at[i, 1]),
            (self.zs.at[i], self.zr.at[i]),
        ]
        self.copies = [
            pltpu.make_async_remote_copy(
                src_ref=source,
                dst_ref=target,
                send_sem=send.at[i, n],
                recv_sem=recv.at[i, n],
                device_id=end,
                device_id_type=MESH,
            )
            for n, ((source, target), end) in enumerate(zip(pairs, ends))
        ]

    def start(self, along):
        self.fields = along
        fx, fy, fz = along
        i = self.step
        quarter = (lane_iota(16) & 15) >> 2
        for k in range(3):
            self.xs[i, k] = fx[k]
        self.copies[0].start()
        self.copies[1].start()
        for side, offset in ((0, 128 - 12), (1, 0)):
            rolled = [
                pltpu.roll(fy[k], (offset + 4 * k) % 128, 1) if (offset + 4 * k) % 128 else fy[k]
                for k in range(3)
            ]
            self.ys[i, side] = jnp.where(
                quarter == 0, rolled[0], jnp.where(quarter == 1, rolled[1], rolled[2])
            )
            self.copies[2 + side].start()
        for k in range(3):
            self.zs[i, k] = fz[k]
        self.copies[4].start()

    def finish(self):
        x, y, a = self.me
        fx, fy, fz = self.fields
        i = self.step
        for copy in self.copies:
            copy.wait()
        for k in range(3):
            self.xb[k, 0:8, :] = jnp.where(x > 0, self.xl[i, k], 0.0)
            self.xb[k, 8:24, :] = fx[k]
            self.xb[k, 24:32, :] = jnp.where(x < GX - 1, self.xr[i, k], 0.0)
        dx = [along_x(self.xb.at[k]) for k in range(3)]
        low = jnp.where(y > 0, self.yr[i, 0], 0.0)
        high = jnp.where(y < GY - 1, self.yr[i, 1], 0.0)
        dy = [along_y(fy[k], k, low, high) for k in range(3)]
        dz = []
        for k in range(3):
            other = self.zr[i, k]
            dz.append(
                along_z(fz[k], jnp.where(a > 0, other, 0.0), jnp.where(a == 0, other, 0.0))
            )
        return dx, dy, dz


def new_velocity(velocity, diffs, factor):
    dx, dy, dz = diffs
    return [velocity[k] + (dx[k] + dy[k] + dz[k]) * factor for k in range(3)]


def strain_rates(diffs):
    dx, dy, dz = diffs
    return [dx[0], dy[1], dz[2], dy[2] + dz[1], dx[2] + dz[0], dx[1] + dy[0]]


def new_stress(stress, strain, stiffness):
    return [
        stress[row]
        + time_step
        * ordered_sum([stiffness[upper(row, col)] * strain[col] for col in range(6)])
        for row in range(6)
    ]


def stress_parts(stress):
    return tuple([stress[i] for i in which] for which in (STRESS_X, STRESS_Y, STRESS_Z))


def entries_of(parts, even):
    out = []
    for i in range(21):
        entry = sparse(FROM_PARTS[i], parts)
        if EVEN[i].any():
            constant = jnp.concatenate([even[i], even[i]], axis=0)
            entry = constant if entry is None else entry + constant
        out.append(entry)
    return out


def main_kernel(*refs):
    given, outs, refs = refs[:8], refs[8:10], refs[10:]
    held, refs = refs[:8], refs[8:]
    angles, table, seeds, even, packed, from_row, from_lane, partial = refs[:8]
    refs = refs[8:]
    fields, arrived, first, first_in, second, second_in, stiff, waves = refs[:8]
    load_sem, out_sem = refs[8:10]
    rs_send, rs_recv, p1_send, p1_recv, p2_send, p2_recv = refs[10:16]
    halo_refs = refs[16:]
    stores = [
        pltpu.make_async_copy(stiff, outs[0], out_sem.at[0]),
        pltpu.make_async_copy(waves.at[0:48], outs[1].at[0:48], out_sem.at[1]),
        pltpu.make_async_copy(waves.at[48:144], outs[1].at[48:144], out_sem.at[2]),
    ]

    loads = [pltpu.make_async_copy(given[i], held[i], load_sem.at[i]) for i in range(8)]
    for load in loads:
        load.start()
    euler, crystal, orient, weight, cell_map, density, velocity, stress = held
    x, y, a = lax.axis_index("gx"), lax.axis_index("gy"), lax.axis_index("ga")
    barrier = pltpu.get_barrier_semaphore()
    ends = [((x + d) % GX, y, a) for d in range(1, GX)]
    ends += [(x, (y + d) % GY, a) for d in range(1, GY)]
    ends += [(x, y, 1 - a)]
    for end in ends:
        pl.semaphore_signal(barrier, inc=1, device_id=end, device_id_type=MESH)

    loads[0].wait()
    loads[1].wait()
    prepare_table(euler, crystal, angles, table, seeds, even)
    for i in range(2, 5):
        loads[i].wait()
    prepare_cells(orient, weight, cell_map, packed, from_row, from_lane)

    halos = [Halo(step, halo_refs, (x, y, a)) for step in range(2 * STEPS)]
    half = [
        pltpu.make_async_remote_copy(
            src_ref=partial.at[pl.ds(i * 8, 8), 0 : PARTS + 1],
            dst_ref=arrived.at[pl.ds(i * 8, 8), 0 : PARTS + 1],
            send_sem=rs_send.at[i],
            recv_sem=rs_recv.at[i],
            device_id=(x, y, 1 - a),
            device_id_type=MESH,
        )
        for i in range(2)
    ]
    to_brick = {}
    for row in range(16):
        d = (row + NEAR) % GX
        if d:
            to_brick[row] = pltpu.make_async_remote_copy(
                src_ref=first.at[row, 0:PARTS],
                dst_ref=first_in.at[x, 0:PARTS],
                send_sem=p1_send.at[d - 1],
                recv_sem=p1_recv.at[d - 1],
                device_id=((x + d) % GX, y, a),
                device_id_type=MESH,
            )

    def sums_of(start):
        return grain_sums(table, seeds, packed, from_row, from_lane, start)

    def other_half(i):
        sums = sums_of(i * 8)
        for c in range(PARTS + 1):
            partial[i * 8 : i * 8 + 8, c, :] = sums[c]

    def own_half(i):
        sums = sums_of(16 + i * 8)
        half[i].wait()
        rows = slice(i * 8, i * 8 + 8)
        gain = 1.0 / (sums[PARTS] + arrived[rows, PARTS, :])
        for c in range(PARTS):
            first[rows, c, :] = (sums[c] + arrived[rows, c, :]) * gain
        for row in range(i * 8, i * 8 + 8):
            if row in to_brick:
                to_brick[row].start()

    other_half(0)
    for i in range(5, 8):
        loads[i].wait()
    for z in range(8):
        lanes = slice(z * 16, z * 16 + 16)
        fields[0:96, lanes] = stress[pl.ds(z, 96, stride=8), :]
        fields[96:144, lanes] = velocity[pl.ds(z, 48, stride=8), :]
        fields[144:160, lanes] = density[pl.ds(z, 16, stride=8), :]
    stresses = [fields[i * 16 : i * 16 + 16, :] for i in range(6)]
    pl.semaphore_wait(barrier, len(ends))
    half[0].start()
    halos[0].start(stress_parts(stresses))
    other_half(1)
    half[1].start()
    own_half(0)
    factor = time_step / fields[144:160, :]
    velocities = [fields[96 + k * 16 : 112 + k * 16, :] for k in range(3)]
    velocities = new_velocity(velocities, halos[0].finish(), factor)
    for k in range(3):
        fields[96 + k * 16 : 112 + k * 16, :] = velocities[k]
    fields[144:160, :] = factor
    halos[1].start((velocities,) * 3)
    own_half(1)
    velocities = [fields[96 + k * 16 : 112 + k * 16, :] for k in range(3)]
    halos[1].fields = (velocities,) * 3
    strain = strain_rates(halos[1].finish())
    for i in range(6):
        fields[160 + i * 16 : 176 + i * 16, :] = strain[i]
    first_in[x, 0:PARTS, :] = first[GX - NEAR, 0:PARTS, :]
    for copy in to_brick.values():
        copy.wait()

    for p in range(2):
        for c in range(PARTS):
            block = first_in[p * 8 : p * 8 + 8, c, :]
            second[:, p, c, :] = block_swap(block, False)
    to_y = []
    for d in range(1, GY):
        target = (y + d) % GY
        copy = pltpu.make_async_remote_copy(
            src_ref=second.at[target, :, 0:PARTS],
            dst_ref=second_in.at[y, :, 0:PARTS],
            send_sem=p2_send.at[d - 1],
            recv_sem=p2_recv.at[d - 1],
            device_id=(x, target, a),
            device_id_type=MESH,
        )
        copy.start()
        to_y.append(copy)
    for p in range(2):
        second_in[y, p, 0:PARTS, :] = second[y, p, 0:PARTS, :]
    for copy in to_y:
        copy.wait()
    parts = []
    for c in range(PARTS):
        parts.append(
            jnp.concatenate([block_swap(second_in[:, p, c, :], True) for p in range(2)], axis=0)
        )
    for i, entry in enumerate(entries_of(parts, even)):
        stiff[i] = entry

    strain = [fields[160 + i * 16 : 176 + i * 16, :] for i in range(6)]
    stresses = [fields[i * 16 : i * 16 + 16, :] for i in range(6)]
    stresses = new_stress(stresses, strain, stiff)
    halos[2].start(stress_parts(stresses))
    stores[0].start()
    factor = fields[144:160, :]
    velocities = [fields[96 + k * 16 : 112 + k * 16, :] for k in range(3)]
    velocities = new_velocity(velocities, halos[2].finish(), factor)
    halos[3].start((velocities,) * 3)
    for k in range(3):
        waves[k * 16 : k * 16 + 16, :] = velocities[k]
    stores[1].start()
    strain = strain_rates(halos[3].finish())
    stresses = new_stress(stresses, strain, stiff)
    for k in range(6):
        waves[48 + k * 16 : 64 + k * 16, :] = stresses[k]
    stores[2].start()
    for store in stores:
        store.wait()


def layout_kernel(
    stiff_in, waves_in, stiff_out, velocity_out, stress_out,
    stiff, waves, stiff_held, velocity_held, stress_held, sems, load_sems,
):
    loads = [
        pltpu.make_async_copy(waves_in, waves, load_sems.at[0]),
        pltpu.make_async_copy(stiff_in, stiff, load_sems.at[1]),
    ]
    for load in loads:
        load.start()
    loads[0].wait()
    copies = []

    def send(source, target):
        copies.append(pltpu.make_async_copy(source, target, sems.at[len(copies)]))
        copies[-1].start()

    for z in range(8):
        lanes = slice(z * 16, z * 16 + 16)
        stress_held[pl.ds(z, 96, stride=8), :] = waves[48:144, lanes]
        velocity_held[pl.ds(z, 48, stride=8), :] = waves[0:48, lanes]
    send(stress_held, stress_out)
    send(velocity_held, velocity_out)
    loads[1].wait()
    for row in range(16):
        turned = jnp.transpose(stiff[:, row, :], (1, 0))
        for z in range(8):
            stiff_held[pl.ds(row * 128 + z, 16, stride=8), :] = turned[z * 16 : z * 16 + 16, :21]
        if row % 4 == 3:
            rows = pl.ds((row - 3) * 128, 512)
            send(stiff_held.at[rows, :], stiff_out.at[rows, :])
    for copy in copies:
        copy.wait()


def on_device(euler_table, crystal, orient, weight, cell_map, density, velocity, stress):
    anywhere = pl.BlockSpec(memory_space=pl.ANY)
    operands = (
        euler_table,
        crystal,
        orient.reshape(512, 128),
        weight.reshape(GRAINS, 4096),
        cell_map.reshape(32, 128),
        density.transpose(0, 2, 1).reshape(128, 16),
        velocity.transpose(0, 1, 3, 2).reshape(384, 16),
        stress.transpose(0, 1, 3, 2).reshape(768, 16),
    )
    scratch = [
        (pltpu.SMEM if i == 1 else pltpu.VMEM)(array.shape, array.dtype)
        for i, array in enumerate(operands)
    ]
    scratch += [
        pltpu.VMEM((48, 128), F32),
        pltpu.VMEM((32, 128), I32),
        pltpu.VMEM((PARTS, 8, 128), F32),
        pltpu.VMEM((21, 8, 128), F32),
        pltpu.VMEM((512, 128), I32),
        pltpu.VMEM((32, 128), I32),
        pltpu.VMEM((32, 128), I32),
        pltpu.VMEM((16, ROWS, 128), F32),
        pltpu.VMEM((256, 128), F32),
        pltpu.VMEM((16, ROWS, 128), F32),
        pltpu.VMEM((16, ROWS, 128), F32),
        pltpu.VMEM((16, ROWS, 128), F32),
        pltpu.VMEM((8, 2, ROWS, 128), F32),
        pltpu.VMEM((8, 2, ROWS, 128), F32),
    ]
    small = (jax.ShapeDtypeStruct((21, 16, 128), F32), jax.ShapeDtypeStruct((144, 128), F32))
    small_held = [pltpu.VMEM(array.shape, F32) for array in small]
    scratch += small_held
    for count in (8, 3, 2, 2, 15, 15, 7, 7):
        scratch.append(pltpu.SemaphoreType.DMA((count,)))
    steps = 2 * STEPS
    scratch += [
        pltpu.VMEM((steps, 3, 16, 128), F32),
        pltpu.VMEM((steps, 3, 8, 128), F32),
        pltpu.VMEM((steps, 3, 8, 128), F32),
        pltpu.VMEM((3, 32, 128), F32),
        pltpu.VMEM((steps, 2, 16, 128), F32),
        pltpu.VMEM((steps, 2, 16, 128), F32),
        pltpu.VMEM((steps, 3, 16, 128), F32),
        pltpu.VMEM((steps, 3, 16, 128), F32),
        pltpu.SemaphoreType.DMA((steps, 5)),
        pltpu.SemaphoreType.DMA((steps, 5)),
    ]
    found = pl.pallas_call(
        main_kernel,
        out_shape=small,
        in_specs=[anywhere] * 8,
        out_specs=(anywhere, anywhere),
        scratch_shapes=scratch,
        compiler_params=pltpu.CompilerParams(
            collective_id=0, has_side_effects=True, vmem_limit_bytes=VMEM_LIMIT
        ),
        name="relay_and_steps",
    )(*operands)
    shapes = ((2048, 21), (384, 16), (768, 16))
    stiffness, velocity, stress = pl.pallas_call(
        layout_kernel,
        out_shape=tuple(jax.ShapeDtypeStruct(shape, F32) for shape in shapes),
        in_specs=[anywhere, anywhere],
        out_specs=(anywhere,) * 3,
        scratch_shapes=small_held
        + [pltpu.VMEM(shape, F32) for shape in shapes]
        + [pltpu.SemaphoreType.DMA((6,)), pltpu.SemaphoreType.DMA((2,))],
        compiler_params=pltpu.CompilerParams(vmem_limit_bytes=VMEM_LIMIT),
        name="layouts",
    )(*found)
    return (
        stiffness.reshape(16, 16, 8, 21).transpose(3, 0, 1, 2),
        velocity.reshape(3, 16, 8, 16).transpose(0, 1, 3, 2),
        stress.reshape(6, 16, 8, 16).transpose(0, 1, 3, 2),
    )


def solution(mesh):
    fields = P(None, "gx", "gy", "ga")
    return jax.shard_map(
        on_device,
        mesh=mesh,
        in_specs=(
            P(),
            P(),
            P("ga", "gx", "gy", None),
            P("ga", "gx", "gy", None),
            P("gx", "gy", None),
            P("gx", "gy", "ga"),
            fields,
            fields,
        ),
        out_specs=(fields, fields, fields),
        check_vma=False,
    )
```

```python
import jax
import jax.numpy as jnp
import numpy as np
from jax import lax
from jax.experimental import pallas as pl
from jax.experimental.pallas import tpu as pltpu
from jax.sharding import PartitionSpec as P

MESH = pl.DeviceIdType.MESH
STEPS = 2
weights = (0.8, -0.2, 4.0 / 105.0, -1.0 / 280.0)
time_step = 0.2
voigt_pairs = ((0, 0), (1, 1), (2, 2), (1, 2), (0, 2), (0, 1))
upper_pairs = [(row, col) for row in range(6) for col in range(row, 6)]
F32, I32 = jnp.float32, jnp.int32
STRESS_X, STRESS_Y, STRESS_Z = (0, 5, 4), (5, 1, 3), (4, 3, 2)
GX, GY, GA = 16, 8, 2
GRAINS = 16
PARTS = 19
ROWS = 24
STEP = 1 << 19
LEAST = 76
VMEM_LIMIT = 56 * 1024 * 1024
FIRST = 5
NEAR = 4


def upper(first, second):
    return upper_pairs.index((min(first, second), max(first, second)))


def ordered_sum(terms):
    total = terms[0]
    for term in terms[1:]:
        total = total + term
    return total


def entry_map(rotation):
    bond = np.zeros((6, 6))
    for i, (p, q) in enumerate(voigt_pairs):
        for j, (k, l) in enumerate(voigt_pairs):
            bond[i, j] = rotation[p, k] * rotation[q, l]
            if k != l:
                bond[i, j] += rotation[p, l] * rotation[q, k]
    image = np.zeros((21, 21))
    for n, (row, col) in enumerate(upper_pairs):
        unit = np.zeros((6, 6))
        unit[row, col] = unit[col, row] = 1.0
        turned = bond @ unit @ bond.T
        image[:, n] = [turned[i, j] for i, j in upper_pairs]
    return image


def turn(axis, angle):
    i, j = (axis + 1) % 3, (axis + 2) % 3
    out = np.eye(3)
    out[i, i] = out[j, j] = np.cos(angle)
    out[j, i] = np.sin(angle)
    out[i, j] = -out[j, i]
    return out


def harmonic_parts():
    size = np.sqrt([(1.0 + (r > 2)) * (1 + (c > 2)) * (1 + (r != c)) for r, c in upper_pairs])
    spins = []
    for axis in range(3):
        spin = np.zeros((21, 21))
        for n in range(16):
            angle = 2 * np.pi * n / 16
            image = size[:, None] * entry_map(turn(axis, angle)) / size
            spin += sum(m * np.sin(m * angle) for m in range(1, 5)) / 8 * image
        spins.append(spin)
    unit = np.eye(21)
    square = -(spins[0] @ spins[0] + spins[1] @ spins[1] + spins[2] @ spins[2])
    level = spins[2] @ spins[2]
    flat = unit
    for m in range(1, 5):
        flat = flat @ (unit + level / m**2)
    chosen = {0: (0, 1), 2: (upper(2, 2), upper(0, 1)), 4: (upper(2, 2),)}
    parts = []
    for degree, seeds in chosen.items():
        keep = flat
        for other in (0, 2, 4):
            if other != degree:
                first, last = degree * (degree + 1), other * (other + 1)
                keep = keep @ (square - last * unit) / (first - last)
        heads = []
        for seed in seeds:
            head = keep[:, seed]
            for former in heads:
                head = head - former * (former @ head)
            heads.append(head / np.linalg.norm(head))
            chain = [heads[-1]]
            for m in range(degree):
                step = spins[1] @ chain[m]
                if m:
                    step = step - chain[m - 1] * (chain[m - 1] @ step)
                chain.append(step / np.linalg.norm(step))
            part = [chain[0]]
            for m in range(1, degree + 1):
                part += [chain[m], spins[2] @ chain[m] / m]
            parts.append(np.stack(part, axis=1))
    basis = np.concatenate(parts[2:], axis=1)
    even = np.concatenate(parts[:2], axis=1)
    quarter = basis.T @ (size[:, None] * entry_map(turn(1, np.pi / 2)) / size) @ basis
    tables = (basis.T * size, basis / size[:, None], (even @ even.T) / size[:, None] * size, quarter)
    return [np.round(table, 9) for table in tables]


TO_PARTS, FROM_PARTS, EVEN, QUARTER = harmonic_parts()
BLOCKS = ((0, 2), (5, 2), (10, 4))


def sparse(row, values):
    terms = []
    for k in range(len(values)):
        factor = float(row[k])
        if factor:
            terms.append(values[k] if factor == 1 else -values[k] if factor == -1 else factor * values[k])
    return ordered_sum(terms) if terms else None


def quarter_turn(parts, matrix):
    out = []
    for start, degree in BLOCKS:
        stop = start + 2 * degree + 1
        out += [sparse(matrix[i, start:stop], parts[start:stop]) for i in range(start, stop)]
    return out


def about_z(parts, cos, sin):
    out = []
    for start, degree in BLOCKS:
        out.append(parts[start] if cos[0] is None else parts[start] * cos[0])
        for m in range(1, degree + 1):
            a, b = parts[start + 2 * m - 1], parts[start + 2 * m]
            out += [a * cos[m] - b * sin[m], a * sin[m] + b * cos[m]]
    return out


def multiples(cos, sin):
    twice = cos + cos
    cos, sin = [None, cos, twice * cos - 1.0], [None, sin, twice * sin]
    for m in (3, 4):
        cos.append(twice * cos[m - 1] - cos[m - 2])
        sin.append(twice * sin[m - 1] - sin[m - 2])
    return cos, sin


def lane_pick(row, index):
    return jnp.take_along_axis(row, index, axis=1, mode="promise_in_bounds")


def sublane_pick(block, index):
    return jnp.take_along_axis(block, index, axis=0, mode="promise_in_bounds")


def tree(values, masks):
    for mask in masks:
        values = [
            jnp.where(mask, values[2 * i + 1], values[2 * i]) for i in range(len(values) // 2)
        ]
    return values[0]


def lane_iota(rows):
    return lax.broadcasted_iota(I32, (rows, 128), 1)


def row_iota(rows):
    return lax.broadcasted_iota(I32, (rows, 128), 0)


def angle_field(angle):
    cos, sin = jnp.cos(angle), jnp.sin(angle)
    back = cos < 0.0
    tangent = jnp.where(back, -sin, sin) / (1.0 + jnp.abs(cos))
    whole = jnp.floor(tangent * STEP + 0.5).astype(I32)
    return jnp.clip(whole, -STEP, STEP - 1) * 2 + back.astype(I32)


def cos_sin(field):
    tangent = field.astype(F32) * (0.5 / STEP)
    square = tangent * tangent
    below = 1.0 + square
    rough = pl.reciprocal(below, approx=True)
    fine = rough * (2.0 - below * rough)
    fine = jnp.where((field & 1) == 1, -fine, fine)
    return (1.0 - square) * fine, (tangent + tangent) * fine


def prepare_table(euler, crystal, angles, table, seeds, even):
    for j in range(16):
        angles[pl.ds(j, 3, stride=16), :] = euler[:, j * 128 : (j + 1) * 128]
    turns = [angle_field(angles[k * 16 : k * 16 + 16, :]) for k in range(3)]
    last = turns[2] + 2 * STEP
    table[0:16, :] = turns[0] * 2048 + (last >> 11)
    table[16:32, :] = turns[1] * 2048 + (last & 2047)
    values = [jnp.full((8, 128), crystal[i], F32) for i in range(21)]
    for i in range(PARTS):
        seeds[i] = sparse(TO_PARTS[i], values)
    for i in range(21):
        found = sparse(EVEN[i], values)
        even[i] = jnp.zeros((8, 128), F32) if found is None else found


def prepare_cells(orient, weight, cell_map, packed, from_row, from_lane):
    for j in range(32):
        mass = (weight[:, j * 128 : (j + 1) * 128].astype(F32) * 2048.0).astype(I32)
        chosen = orient[pl.ds(j, GRAINS, stride=32), :]
        power = ordered_sum([(mass >= bound).astype(I32) for bound in (256, 512, 1024, 2048)])
        code = power * 128 + (mass >> power) - (128 + LEAST)
        packed[pl.ds(j, GRAINS, stride=32), :] = chosen * 512 + code
    for quad in range(GRAINS // 4):
        four = [packed[(4 * quad + k) * 32 : (4 * quad + k) * 32 + 32, :] for k in range(4)]
        words = (four[0] + ((four[3] & 4095) << 20), four[1] + ((four[3] >> 12) << 20), four[2])
        for k in range(3):
            packed[(3 * quad + k) * 32 : (3 * quad + k) * 32 + 32, :] = words[k]
    me_x, me_a = lax.axis_index("gx"), lax.axis_index("ga")
    slot = cell_map[...]
    depth = slot & 15
    own = ((depth >> 3) == me_a).astype(I32)
    to_row = own * 16 + (((slot >> 8) - me_x + (GX - NEAR)) & 15)
    to_lane = ((slot >> 4) & 15) * 8 + (depth & 7)
    rows, lanes = row_iota(32), row_iota(128)
    here = lane_iota(32).astype(F32)
    found = jnp.zeros((64, 128), F32)
    for j in range(32):
        hit = rows == jnp.broadcast_to(to_row[j : j + 1, :], (32, 128))
        left = jnp.concatenate(
            [jnp.where(hit, float(j), 0.0), jnp.where(hit, here, 0.0)], axis=0
        ).astype(jnp.bfloat16)
        right = jnp.where(lanes == jnp.broadcast_to(to_lane[j : j + 1, :], (128, 128)), 1.0, 0.0)
        found = found + lax.dot_general(
            left,
            right.astype(jnp.bfloat16),
            (((1,), (1,)), ((), ())),
            preferred_element_type=F32,
        )
    found = (found + 0.5).astype(I32)
    from_row[...] = found[:32]
    from_lane[...] = found[32:]


def grain_sums(table, seeds, packed, from_row, from_lane, block, carry=None):
    quads = GRAINS // 4

    def fetch(step):
        step = jnp.minimum(step, 4 * quads - 1)
        first = lax.rem(step, quads) * 96
        rows = pl.ds(pl.multiple_of(lax.div(step, quads) * 8, 8), 8)
        lane, row = from_lane[rows, :], from_row[rows, :]
        bits = [((row >> bit) & 1) == 1 for bit in range(5)]
        return [
            tree(
                [
                    lane_pick(
                        jnp.broadcast_to(packed[pl.ds(first + k * 32 + j, 1), :], (8, 128)), lane
                    )
                    for j in range(32)
                ],
                bits,
            )
            for k in range(3)
        ]

    def look_up(words):
        low = (1 << 20) - 1
        last = ((words[0] >> 20) & 4095) + ((words[1] >> 20) << 12)
        found = []
        for word in (words[0] & low, words[1] & low, words[2], last):
            spot = (word >> 9) & 127
            bits = [((word >> (16 + bit)) & 1) == 1 for bit in range(4)]
            found.append(word)
            for k in range(2):
                rows = [table[k * 16 + h : k * 16 + h + 1, :] for h in range(16)]
                found.append(
                    tree([lane_pick(jnp.broadcast_to(r, (8, 128)), spot) for r in rows], bits)
                )
        return found

    def add(word, one, two, sums):
        code = (word & 511) + LEAST
        mass = ((128 + (code & 127)) << (code >> 7)).astype(F32)
        fields = (one >> 11, two >> 11, ((one & 1023) << 11) + (two & 2047) - 2 * STEP)
        turns = [multiples(*cos_sin(field)) for field in fields]
        cos, sin = turns[2]
        cos = [mass] + [mass * value for value in cos[1:]]
        sin = [None] + [mass * value for value in sin[1:]]
        parts = about_z([seeds[i] for i in range(PARTS)], cos, sin)
        parts = quarter_turn(parts, QUARTER.T)
        parts = about_z(parts, *turns[1])
        parts = quarter_turn(parts, QUARTER)
        parts = about_z(parts, *turns[0])
        return [old + new for old, new in zip(sums, parts)] + [sums[PARTS] + mass]

    def absorb(step, carry):
        words, found, sums = carry[:3], carry[3:15], carry[15:]
        after = fetch(step + 2)
        coming = look_up(words)
        for k in range(4):
            sums = add(*found[3 * k : 3 * k + 3], sums)
        return (*after, *coming, *sums)

    if carry is None:
        carry = (*fetch(jnp.int32(1)), *look_up(fetch(jnp.int32(0))))
    sums = (jnp.zeros((8, 128), F32),) * (PARTS + 1)
    begin = block * quads
    out = lax.fori_loop(begin, begin + quads, absorb, (*carry, *sums))
    return out[15:], out[:15]


def block_swap(block, regroup):
    sublane, lane = row_iota(8), lane_iota(8)
    group, place = lane >> 4, lane & 15
    skewed = lane_pick(block, ((group + sublane) & 7) * 16 + place)
    skewed = sublane_pick(skewed, (sublane - group) & 7)
    if regroup:
        y, z = lane & 15, lane >> 4
        group, place = y >> 1, (y & 1) * 8 + z
    return lane_pick(skewed, ((sublane - group) & 7) * 16 + place)


def along_y(field, k, low, high):
    y = lane_iota(16) & 15
    low = pltpu.roll(low, 128 - (4 + 4 * k), 1)
    high = pltpu.roll(high, 16 - 4 * k, 1)
    total = None
    for m in range(1, 5):
        up = pltpu.roll(jnp.where(y < m, high, field), 128 - m, 1)
        down = pltpu.roll(jnp.where(y >= 16 - m, low, field), m, 1)
        term = weights[m - 1] * (up - down)
        total = term if total is None else total + term
    return total


def along_z(field, low, high):
    z = lane_iota(16) >> 4
    total = None
    for m in range(1, 5):
        up = pltpu.roll(jnp.where(z < m, high, field), 128 - 16 * m, 1)
        down = pltpu.roll(jnp.where(z >= 8 - m, low, field), 16 * m, 1)
        term = weights[m - 1] * (up - down)
        total = term if total is None else total + term
    return total


def along_x(padded):
    total = None
    for m in range(1, 5):
        term = weights[m - 1] * (padded[8 + m : 24 + m, :] - padded[8 - m : 24 - m, :])
        total = term if total is None else total + term
    return total


class Halo:
    def __init__(self, step, refs, me):
        self.step, self.me = step, me
        self.xs, self.xl, self.xr, self.xb, self.ys, self.yr, self.zs, self.zr, send, recv = refs
        x, y, a = me
        ends = [((x + 1) % GX, y, a), ((x + GX - 1) % GX, y, a)]
        ends += [(x, (y + 1) % GY, a), (x, (y + GY - 1) % GY, a), (x, y, 1 - a)]
        i = step
        pairs = [
            (self.xs.at[i, :, 8:16], self.xl.at[i]),
            (self.xs.at[i, :, 0:8], self.xr.at[i]),
            (self.ys.at[i, 0], self.yr.at[i, 0]),
            (self.ys.at[i, 1], self.yr.at[i, 1]),
            (self.zs.at[i], self.zr.at[i]),
        ]
        self.copies = [
            pltpu.make_async_remote_copy(
                src_ref=source,
                dst_ref=target,
                send_sem=send.at[i, n],
                recv_sem=recv.at[i, n],
                device_id=end,
                device_id_type=MESH,
            )
            for n, ((source, target), end) in enumerate(zip(pairs, ends))
        ]

    def start_y(self, fields):
        self.along_y = fields
        i = self.step
        quarter = (lane_iota(16) & 15) >> 2
        for side, offset in ((0, 128 - 12), (1, 0)):
            rolled = [
                pltpu.roll(fields[k], (offset + 4 * k) % 128, 1) if offset + 4 * k else fields[k]
                for k in range(3)
            ]
            self.ys[i, side] = jnp.where(
                quarter == 0, rolled[0], jnp.where(quarter == 1, rolled[1], rolled[2])
            )
            self.copies[2 + side].start()

    def start_x(self, fields):
        self.along_x = fields
        for k in range(3):
            self.xs[self.step, k] = fields[k]
        self.copies[0].start()
        self.copies[1].start()

    def start_z(self, fields):
        self.along_z = fields
        for k in range(3):
            self.zs[self.step, k] = fields[k]
        self.copies[4].start()

    def start(self, along):
        fx, fy, fz = along
        self.start_y(fy)
        self.start_x(fx)
        self.start_z(fz)

    def finish(self):
        x, y, a = self.me
        i = self.step
        self.copies[4].wait()
        dz = []
        for k in range(3):
            other = self.zr[i, k]
            low, high = jnp.where(a > 0, other, 0.0), jnp.where(a == 0, other, 0.0)
            dz.append(along_z(self.along_z[k], low, high))
        self.copies[0].wait()
        self.copies[1].wait()
        for k in range(3):
            self.xb[k, 0:8, :] = jnp.where(x > 0, self.xl[i, k], 0.0)
            self.xb[k, 8:24, :] = self.along_x[k]
            self.xb[k, 24:32, :] = jnp.where(x < GX - 1, self.xr[i, k], 0.0)
        dx = [along_x(self.xb.at[k]) for k in range(3)]
        self.copies[2].wait()
        self.copies[3].wait()
        low = jnp.where(y > 0, self.yr[i, 0], 0.0)
        high = jnp.where(y < GY - 1, self.yr[i, 1], 0.0)
        dy = [along_y(self.along_y[k], k, low, high) for k in range(3)]
        return dx, dy, dz


def new_velocity(velocity, diffs, factor):
    dx, dy, dz = diffs
    return [velocity[k] + (dx[k] + dy[k] + dz[k]) * factor for k in range(3)]


def strain_rates(diffs):
    dx, dy, dz = diffs
    return [dx[0], dy[1], dz[2], dy[2] + dz[1], dx[2] + dz[0], dx[1] + dy[0]]


def new_component(stress, strain, stiffness, row):
    change = ordered_sum([stiffness[upper(row, col)] * strain[col] for col in range(6)])
    return stress[row] + time_step * change


def new_stress(stress, strain, stiffness):
    return [new_component(stress, strain, stiffness, row) for row in range(6)]


def stress_parts(stress):
    return tuple([stress[i] for i in which] for which in (STRESS_X, STRESS_Y, STRESS_Z))


def entries_of(parts, even):
    out = []
    for i in range(21):
        entry = sparse(FROM_PARTS[i], parts)
        if EVEN[i].any():
            constant = jnp.concatenate([even[i], even[i]], axis=0)
            entry = constant if entry is None else entry + constant
        out.append(entry)
    return out


def main_kernel(*refs):
    given, outs, refs = refs[:8], refs[8:10], refs[10:]
    held, refs = refs[:8], refs[8:]
    angles, table, seeds, even, packed, from_row, from_lane, partial = refs[:8]
    refs = refs[8:]
    fields, arrived, first, first_in, second, second_in, stiff, waves = refs[:8]
    load_sem, out_sem = refs[8:10]
    rs_send, rs_recv, p1_send, p1_recv, p2_send, p2_recv = refs[10:16]
    halo_refs = refs[16:]
    stores = [
        pltpu.make_async_copy(stiff, outs[0], out_sem.at[0]),
        pltpu.make_async_copy(waves.at[0:48], outs[1].at[0:48], out_sem.at[1]),
        pltpu.make_async_copy(waves.at[48:144], outs[1].at[48:144], out_sem.at[2]),
    ]

    loads = [pltpu.make_async_copy(given[i], held[i], load_sem.at[i]) for i in range(8)]
    for load in loads:
        load.start()
    euler, crystal, orient, weight, cell_map, density, velocity, stress = held
    x, y, a = lax.axis_index("gx"), lax.axis_index("gy"), lax.axis_index("ga")
    barrier = pltpu.get_barrier_semaphore()
    ends = [((x + d) % GX, y, a) for d in range(1, GX)]
    ends += [(x, (y + d) % GY, a) for d in range(1, GY)]
    ends += [(x, y, 1 - a)]
    for end in ends:
        pl.semaphore_signal(barrier, inc=1, device_id=end, device_id_type=MESH)

    loads[0].wait()
    loads[1].wait()
    prepare_table(euler, crystal, angles, table, seeds, even)
    for i in range(2, 5):
        loads[i].wait()
    prepare_cells(orient, weight, cell_map, packed, from_row, from_lane)

    halos = [Halo(step, halo_refs, (x, y, a)) for step in range(2 * STEPS)]
    half = [
        pltpu.make_async_remote_copy(
            src_ref=partial.at[pl.ds(i * 8, 8), 0 : PARTS + 1],
            dst_ref=arrived.at[pl.ds(i * 8, 8), 0 : PARTS + 1],
            send_sem=rs_send.at[i],
            recv_sem=rs_recv.at[i],
            device_id=(x, y, 1 - a),
            device_id_type=MESH,
        )
        for i in range(2)
    ]
    def slot_of(d):
        return (GX - d - FIRST) % GX

    to_brick = {}
    for row in range(16):
        d = (row + NEAR) % GX
        if d:
            to_brick[row] = pltpu.make_async_remote_copy(
                src_ref=first.at[row, 0:PARTS],
                dst_ref=first_in.at[slot_of(d), 0:PARTS],
                send_sem=p1_send.at[d - 1],
                recv_sem=p1_recv.at[d - 1],
                device_id=((x + d) % GX, y, a),
                device_id_type=MESH,
            )

    carry = [None]

    def sums_of(block):
        sums, carry[0] = grain_sums(table, seeds, packed, from_row, from_lane, block, carry[0])
        return sums

    def other_half(i):
        sums = sums_of(i)
        for c in range(PARTS + 1):
            partial[i * 8 : i * 8 + 8, c, :] = sums[c]

    def own_half(i):
        sums = sums_of(2 + i)
        half[i].wait()
        rows = slice(i * 8, i * 8 + 8)
        gain = 1.0 / (sums[PARTS] + arrived[rows, PARTS, :])
        for c in range(PARTS):
            first[rows, c, :] = (sums[c] + arrived[rows, c, :]) * gain
        for row in range(i * 8, i * 8 + 8):
            if row in to_brick:
                to_brick[row].start()

    other_half(0)
    for i in range(5, 8):
        loads[i].wait()
    for z in range(8):
        lanes = slice(z * 16, z * 16 + 16)
        fields[0:96, lanes] = stress[pl.ds(z, 96, stride=8), :]
        fields[96:144, lanes] = velocity[pl.ds(z, 48, stride=8), :]
        fields[144:160, lanes] = density[pl.ds(z, 16, stride=8), :]
    stresses = [fields[i * 16 : i * 16 + 16, :] for i in range(6)]
    pl.semaphore_wait(barrier, len(ends))
    half[0].start()
    halos[0].start(stress_parts(stresses))
    other_half(1)
    half[1].start()
    own_half(0)
    factor = time_step / fields[144:160, :]
    velocities = [fields[96 + k * 16 : 112 + k * 16, :] for k in range(3)]
    velocities = new_velocity(velocities, halos[0].finish(), factor)
    for k in range(3):
        fields[96 + k * 16 : 112 + k * 16, :] = velocities[k]
    fields[144:160, :] = factor
    halos[1].start((velocities,) * 3)
    own_half(1)

    to_y = []

    def forward(g):
        for c in range(PARTS):
            block = first_in[g * 8 : g * 8 + 8, c, :]
            second[:, g, c, :] = block_swap(block, False)
        for d in range(1, GY):
            target = (y + d) % GY
            copy = pltpu.make_async_remote_copy(
                src_ref=second.at[target, g, 0:PARTS],
                dst_ref=second_in.at[y, g, 0:PARTS],
                send_sem=p2_send.at[g * (GY - 1) + d - 1],
                recv_sem=p2_recv.at[g * (GY - 1) + d - 1],
                device_id=(x, target, a),
                device_id_type=MESH,
            )
            copy.start()
            to_y.append(copy)
        second_in[y, g, 0:PARTS, :] = second[y, g, 0:PARTS, :]

    for row in range(8):
        to_brick[row].wait()
    forward(0)
    velocities = [fields[96 + k * 16 : 112 + k * 16, :] for k in range(3)]
    halos[1].along_x = halos[1].along_y = halos[1].along_z = velocities
    strain = strain_rates(halos[1].finish())
    for i in range(6):
        fields[160 + i * 16 : 176 + i * 16, :] = strain[i]
    first_in[slot_of(0), 0:PARTS, :] = first[GX - NEAR, 0:PARTS, :]
    for row in range(8, 16):
        if row in to_brick:
            to_brick[row].wait()
    forward(1)
    for copy in to_y:
        copy.wait()
    parts = []
    for c in range(PARTS):
        rows = [block_swap(second_in[:, g, c, :], True) for g in range(2)]
        parts.append(pltpu.roll(jnp.concatenate(rows, axis=0), (x + FIRST) % GX, 0))
    for i, entry in enumerate(entries_of(parts, even)):
        stiff[i] = entry

    strain = [fields[160 + i * 16 : 176 + i * 16, :] for i in range(6)]
    stresses = [fields[i * 16 : i * 16 + 16, :] for i in range(6)]
    fresh = {}
    for which, begin in (
        (STRESS_Y, halos[2].start_y),
        (STRESS_X, halos[2].start_x),
        (STRESS_Z, halos[2].start_z),
    ):
        for row in which:
            if row not in fresh:
                fresh[row] = new_component(stresses, strain, stiff, row)
        begin([fresh[row] for row in which])
    stresses = [fresh[row] for row in range(6)]
    stores[0].start()
    factor = fields[144:160, :]
    velocities = [fields[96 + k * 16 : 112 + k * 16, :] for k in range(3)]
    velocities = new_velocity(velocities, halos[2].finish(), factor)
    halos[3].start((velocities,) * 3)
    for k in range(3):
        waves[k * 16 : k * 16 + 16, :] = velocities[k]
    stores[1].start()
    strain = strain_rates(halos[3].finish())
    stresses = new_stress(stresses, strain, stiff)
    for k in range(6):
        waves[48 + k * 16 : 64 + k * 16, :] = stresses[k]
    stores[2].start()
    for store in stores:
        store.wait()


def layout_kernel(
    stiff_in, waves_in, stiff_out, velocity_out, stress_out,
    stiff, waves, stiff_held, velocity_held, stress_held, sems, load_sems,
):
    loads = [
        pltpu.make_async_copy(waves_in, waves, load_sems.at[0]),
        pltpu.make_async_copy(stiff_in, stiff, load_sems.at[1]),
    ]
    for load in loads:
        load.start()
    loads[0].wait()
    copies = []

    def send(source, target):
        copies.append(pltpu.make_async_copy(source, target, sems.at[len(copies)]))
        copies[-1].start()

    for z in range(8):
        lanes = slice(z * 16, z * 16 + 16)
        stress_held[pl.ds(z, 96, stride=8), :] = waves[48:144, lanes]
        velocity_held[pl.ds(z, 48, stride=8), :] = waves[0:48, lanes]
    send(stress_held, stress_out)
    send(velocity_held, velocity_out)
    loads[1].wait()
    for row in range(16):
        turned = jnp.transpose(stiff[:, row, :], (1, 0))
        for z in range(8):
            stiff_held[pl.ds(row * 128 + z, 16, stride=8), :] = turned[z * 16 : z * 16 + 16, :21]
        if row % 4 == 3:
            rows = pl.ds((row - 3) * 128, 512)
            send(stiff_held.at[rows, :], stiff_out.at[rows, :])
    for copy in copies:
        copy.wait()


def on_device(euler_table, crystal, orient, weight, cell_map, density, velocity, stress):
    anywhere = pl.BlockSpec(memory_space=pl.ANY)
    operands = (
        euler_table,
        crystal,
        orient.reshape(512, 128),
        weight.reshape(GRAINS, 4096),
        cell_map.reshape(32, 128),
        density.transpose(0, 2, 1).reshape(128, 16),
        velocity.transpose(0, 1, 3, 2).reshape(384, 16),
        stress.transpose(0, 1, 3, 2).reshape(768, 16),
    )
    scratch = [
        (pltpu.SMEM if i == 1 else pltpu.VMEM)(array.shape, array.dtype)
        for i, array in enumerate(operands)
    ]
    scratch += [
        pltpu.VMEM((48, 128), F32),
        pltpu.VMEM((32, 128), I32),
        pltpu.VMEM((PARTS, 8, 128), F32),
        pltpu.VMEM((21, 8, 128), F32),
        pltpu.VMEM((512, 128), I32),
        pltpu.VMEM((32, 128), I32),
        pltpu.VMEM((32, 128), I32),
        pltpu.VMEM((16, ROWS, 128), F32),
        pltpu.VMEM((256, 128), F32),
        pltpu.VMEM((16, ROWS, 128), F32),
        pltpu.VMEM((16, ROWS, 128), F32),
        pltpu.VMEM((16, ROWS, 128), F32),
        pltpu.VMEM((8, 2, ROWS, 128), F32),
        pltpu.VMEM((8, 2, ROWS, 128), F32),
    ]
    small = (jax.ShapeDtypeStruct((21, 16, 128), F32), jax.ShapeDtypeStruct((144, 128), F32))
    small_held = [pltpu.VMEM(array.shape, F32) for array in small]
    scratch += small_held
    for count in (8, 3, 2, 2, 15, 15, 14, 14):
        scratch.append(pltpu.SemaphoreType.DMA((count,)))
    steps = 2 * STEPS
    scratch += [
        pltpu.VMEM((steps, 3, 16, 128), F32),
        pltpu.VMEM((steps, 3, 8, 128), F32),
        pltpu.VMEM((steps, 3, 8, 128), F32),
        pltpu.VMEM((3, 32, 128), F32),
        pltpu.VMEM((steps, 2, 16, 128), F32),
        pltpu.VMEM((steps, 2, 16, 128), F32),
        pltpu.VMEM((steps, 3, 16, 128), F32),
        pltpu.VMEM((steps, 3, 16, 128), F32),
        pltpu.SemaphoreType.DMA((steps, 5)),
        pltpu.SemaphoreType.DMA((steps, 5)),
    ]
    found = pl.pallas_call(
        main_kernel,
        out_shape=small,
        in_specs=[anywhere] * 8,
        out_specs=(anywhere, anywhere),
        scratch_shapes=scratch,
        compiler_params=pltpu.CompilerParams(
            collective_id=0, has_side_effects=True, vmem_limit_bytes=VMEM_LIMIT
        ),
        name="relay_and_steps",
    )(*operands)
    shapes = ((2048, 21), (384, 16), (768, 16))
    stiffness, velocity, stress = pl.pallas_call(
        layout_kernel,
        out_shape=tuple(jax.ShapeDtypeStruct(shape, F32) for shape in shapes),
        in_specs=[anywhere, anywhere],
        out_specs=(anywhere,) * 3,
        scratch_shapes=small_held
        + [pltpu.VMEM(shape, F32) for shape in shapes]
        + [pltpu.SemaphoreType.DMA((6,)), pltpu.SemaphoreType.DMA((2,))],
        compiler_params=pltpu.CompilerParams(vmem_limit_bytes=VMEM_LIMIT),
        name="layouts",
    )(*found)
    return (
        stiffness.reshape(16, 16, 8, 21).transpose(3, 0, 1, 2),
        velocity.reshape(3, 16, 8, 16).transpose(0, 1, 3, 2),
        stress.reshape(6, 16, 8, 16).transpose(0, 1, 3, 2),
    )


def solution(mesh):
    fields = P(None, "gx", "gy", "ga")
    return jax.shard_map(
        on_device,
        mesh=mesh,
        in_specs=(
            P(),
            P(),
            P("ga", "gx", "gy", None),
            P("ga", "gx", "gy", None),
            P("gx", "gy", None),
            P("gx", "gy", "ga"),
            fields,
            fields,
        ),
        out_specs=(fields, fields, fields),
        check_vma=False,
    )
```

```python
import jax
import jax.numpy as jnp
import numpy as np
from jax import lax
from jax.experimental import pallas as pl
from jax.experimental.pallas import tpu as pltpu
from jax.sharding import PartitionSpec as P

MESH = pl.DeviceIdType.MESH
STEPS = 2
weights = (0.8, -0.2, 4.0 / 105.0, -1.0 / 280.0)
time_step = 0.2
voigt_pairs = ((0, 0), (1, 1), (2, 2), (1, 2), (0, 2), (0, 1))
upper_pairs = [(row, col) for row in range(6) for col in range(row, 6)]
F32, I32 = jnp.float32, jnp.int32
STRESS_X, STRESS_Y, STRESS_Z = (0, 5, 4), (5, 1, 3), (4, 3, 2)
GX, GY, GA = 16, 8, 2
GRAINS = 16
PARTS = 19
ROWS = 24
STEP = 1 << 19
LEAST = 76
VMEM_LIMIT = 56 * 1024 * 1024
FIRST = 5
NEAR = 4


def upper(first, second):
    return upper_pairs.index((min(first, second), max(first, second)))


def ordered_sum(terms):
    total = terms[0]
    for term in terms[1:]:
        total = total + term
    return total


def entry_map(rotation):
    bond = np.zeros((6, 6))
    for i, (p, q) in enumerate(voigt_pairs):
        for j, (k, l) in enumerate(voigt_pairs):
            bond[i, j] = rotation[p, k] * rotation[q, l]
            if k != l:
                bond[i, j] += rotation[p, l] * rotation[q, k]
    image = np.zeros((21, 21))
    for n, (row, col) in enumerate(upper_pairs):
        unit = np.zeros((6, 6))
        unit[row, col] = unit[col, row] = 1.0
        turned = bond @ unit @ bond.T
        image[:, n] = [turned[i, j] for i, j in upper_pairs]
    return image


def turn(axis, angle):
    i, j = (axis + 1) % 3, (axis + 2) % 3
    out = np.eye(3)
    out[i, i] = out[j, j] = np.cos(angle)
    out[j, i] = np.sin(angle)
    out[i, j] = -out[j, i]
    return out


def harmonic_parts():
    size = np.sqrt([(1.0 + (r > 2)) * (1 + (c > 2)) * (1 + (r != c)) for r, c in upper_pairs])
    spins = []
    for axis in range(3):
        spin = np.zeros((21, 21))
        for n in range(16):
            angle = 2 * np.pi * n / 16
            image = size[:, None] * entry_map(turn(axis, angle)) / size
            spin += sum(m * np.sin(m * angle) for m in range(1, 5)) / 8 * image
        spins.append(spin)
    unit = np.eye(21)
    square = -(spins[0] @ spins[0] + spins[1] @ spins[1] + spins[2] @ spins[2])
    level = spins[2] @ spins[2]
    flat = unit
    for m in range(1, 5):
        flat = flat @ (unit + level / m**2)
    chosen = {0: (0, 1), 2: (upper(2, 2), upper(0, 1)), 4: (upper(2, 2),)}
    parts = []
    for degree, seeds in chosen.items():
        keep = flat
        for other in (0, 2, 4):
            if other != degree:
                first, last = degree * (degree + 1), other * (other + 1)
                keep = keep @ (square - last * unit) / (first - last)
        heads = []
        for seed in seeds:
            head = keep[:, seed]
            for former in heads:
                head = head - former * (former @ head)
            heads.append(head / np.linalg.norm(head))
            chain = [heads[-1]]
            for m in range(degree):
                step = spins[1] @ chain[m]
                if m:
                    step = step - chain[m - 1] * (chain[m - 1] @ step)
                chain.append(step / np.linalg.norm(step))
            part = [chain[0]]
            for m in range(1, degree + 1):
                part += [chain[m], spins[2] @ chain[m] / m]
            parts.append(np.stack(part, axis=1))
    basis = np.concatenate(parts[2:], axis=1)
    even = np.concatenate(parts[:2], axis=1)
    quarter = basis.T @ (size[:, None] * entry_map(turn(1, np.pi / 2)) / size) @ basis
    tables = (basis.T * size, basis / size[:, None], (even @ even.T) / size[:, None] * size, quarter)
    return [np.round(table, 9) for table in tables]


TO_PARTS, FROM_PARTS, EVEN, QUARTER = harmonic_parts()
BLOCKS = ((0, 2), (5, 2), (10, 4))


def sparse(row, values):
    terms = []
    for k in range(len(values)):
        factor = float(row[k])
        if factor:
            terms.append(values[k] if factor == 1 else -values[k] if factor == -1 else factor * values[k])
    return ordered_sum(terms) if terms else None


def quarter_turn(parts, matrix):
    out = []
    for start, degree in BLOCKS:
        stop = start + 2 * degree + 1
        out += [sparse(matrix[i, start:stop], parts[start:stop]) for i in range(start, stop)]
    return out


def about_z(parts, cos, sin):
    out = []
    for start, degree in BLOCKS:
        out.append(parts[start] if cos[0] is None else parts[start] * cos[0])
        for m in range(1, degree + 1):
            a, b = parts[start + 2 * m - 1], parts[start + 2 * m]
            out += [a * cos[m] - b * sin[m], a * sin[m] + b * cos[m]]
    return out


def multiples(cos, sin):
    twice = cos + cos
    cos, sin = [None, cos, twice * cos - 1.0], [None, sin, twice * sin]
    for m in (3, 4):
        cos.append(twice * cos[m - 1] - cos[m - 2])
        sin.append(twice * sin[m - 1] - sin[m - 2])
    return cos, sin


def lane_pick(row, index):
    return jnp.take_along_axis(row, index, axis=1, mode="promise_in_bounds")


def sublane_pick(block, index):
    return jnp.take_along_axis(block, index, axis=0, mode="promise_in_bounds")


def tree(values, masks):
    for mask in masks:
        values = [
            jnp.where(mask, values[2 * i + 1], values[2 * i]) for i in range(len(values) // 2)
        ]
    return values[0]


def lane_iota(rows):
    return lax.broadcasted_iota(I32, (rows, 128), 1)


def row_iota(rows):
    return lax.broadcasted_iota(I32, (rows, 128), 0)


def angle_field(angle):
    cos, sin = jnp.cos(angle), jnp.sin(angle)
    back = cos < 0.0
    tangent = jnp.where(back, -sin, sin) / (1.0 + jnp.abs(cos))
    whole = jnp.floor(tangent * STEP + 0.5).astype(I32)
    return jnp.clip(whole, -STEP, STEP - 1) * 2 + back.astype(I32)


def cos_sin(field):
    tangent = field.astype(F32) * (0.5 / STEP)
    square = tangent * tangent
    below = 1.0 + square
    rough = pl.reciprocal(below, approx=True)
    fine = rough * (2.0 - below * rough)
    fine = jnp.where((field & 1) == 1, -fine, fine)
    return (1.0 - square) * fine, (tangent + tangent) * fine


def prepare_table(euler, crystal, angles, table, seeds, even):
    for j in range(16):
        angles[pl.ds(j, 3, stride=16), :] = euler[:, j * 128 : (j + 1) * 128]
    turns = [angle_field(angles[k * 16 : k * 16 + 16, :]) for k in range(3)]
    last = turns[2] + 2 * STEP
    table[0:16, :] = turns[0] * 2048 + (last >> 11)
    table[16:32, :] = turns[1] * 2048 + (last & 2047)
    values = [jnp.full((8, 128), crystal[i], F32) for i in range(21)]
    for i in range(PARTS):
        seeds[i] = sparse(TO_PARTS[i], values)
    for i in range(21):
        found = sparse(EVEN[i], values)
        even[i] = jnp.zeros((8, 128), F32) if found is None else found


def prepare_cells(orient, weight, cell_map, packed, from_row, from_lane):
    for j in range(32):
        mass = (weight[:, j * 128 : (j + 1) * 128].astype(F32) * 2048.0).astype(I32)
        chosen = orient[pl.ds(j, GRAINS, stride=32), :]
        power = ordered_sum([(mass >= bound).astype(I32) for bound in (256, 512, 1024, 2048)])
        code = power * 128 + (mass >> power) - (128 + LEAST)
        packed[pl.ds(j, GRAINS, stride=32), :] = chosen * 512 + code
    for quad in range(GRAINS // 4):
        four = [packed[(4 * quad + k) * 32 : (4 * quad + k) * 32 + 32, :] for k in range(4)]
        words = (four[0] + ((four[3] & 4095) << 20), four[1] + ((four[3] >> 12) << 20), four[2])
        for k in range(3):
            packed[(3 * quad + k) * 32 : (3 * quad + k) * 32 + 32, :] = words[k]
    me_x, me_a = lax.axis_index("gx"), lax.axis_index("ga")
    slot = cell_map[...]
    depth = slot & 15
    own = ((depth >> 3) == me_a).astype(I32)
    to_row = own * 16 + (((slot >> 8) - me_x + (GX - NEAR)) & 15)
    to_lane = ((slot >> 4) & 15) * 8 + (depth & 7)
    rows, lanes = row_iota(32), row_iota(128)
    here = lane_iota(32).astype(F32)
    found = jnp.zeros((64, 128), F32)
    for j in range(32):
        hit = rows == jnp.broadcast_to(to_row[j : j + 1, :], (32, 128))
        left = jnp.concatenate(
            [jnp.where(hit, float(j), 0.0), jnp.where(hit, here, 0.0)], axis=0
        ).astype(jnp.bfloat16)
        right = jnp.where(lanes == jnp.broadcast_to(to_lane[j : j + 1, :], (128, 128)), 1.0, 0.0)
        found = found + lax.dot_general(
            left,
            right.astype(jnp.bfloat16),
            (((1,), (1,)), ((), ())),
            preferred_element_type=F32,
        )
    found = (found + 0.5).astype(I32)
    from_row[...] = found[:32]
    from_lane[...] = found[32:]


def grain_sums(table, seeds, packed, from_row, from_lane, block, carry=None):
    quads = GRAINS // 4

    def fetch(step):
        step = jnp.minimum(step, 4 * quads - 1)
        first = lax.rem(step, quads) * 96
        rows = pl.ds(pl.multiple_of(lax.div(step, quads) * 8, 8), 8)
        lane, row = from_lane[rows, :], from_row[rows, :]
        bits = [((row >> bit) & 1) == 1 for bit in range(5)]
        return [
            tree(
                [
                    lane_pick(
                        jnp.broadcast_to(packed[pl.ds(first + k * 32 + j, 1), :], (8, 128)), lane
                    )
                    for j in range(32)
                ],
                bits,
            )
            for k in range(3)
        ]

    def look_up(words):
        low = (1 << 20) - 1
        last = ((words[0] >> 20) & 4095) + ((words[1] >> 20) << 12)
        found = []
        for word in (words[0] & low, words[1] & low, words[2], last):
            spot = (word >> 9) & 127
            bits = [((word >> (16 + bit)) & 1) == 1 for bit in range(4)]
            found.append(word)
            for k in range(2):
                rows = [table[k * 16 + h : k * 16 + h + 1, :] for h in range(16)]
                found.append(
                    tree([lane_pick(jnp.broadcast_to(r, (8, 128)), spot) for r in rows], bits)
                )
        return found

    def add(word, one, two, sums):
        code = (word & 511) + LEAST
        mass = ((128 + (code & 127)) << (code >> 7)).astype(F32)
        fields = (one >> 11, two >> 11, ((one & 1023) << 11) + (two & 2047) - 2 * STEP)
        turns = [multiples(*cos_sin(field)) for field in fields]
        cos, sin = turns[2]
        cos = [mass] + [mass * value for value in cos[1:]]
        sin = [None] + [mass * value for value in sin[1:]]
        parts = about_z([seeds[i] for i in range(PARTS)], cos, sin)
        parts = quarter_turn(parts, QUARTER.T)
        parts = about_z(parts, *turns[1])
        parts = quarter_turn(parts, QUARTER)
        parts = about_z(parts, *turns[0])
        return [old + new for old, new in zip(sums, parts)] + [sums[PARTS] + mass]

    def absorb(step, carry):
        words, found, sums = carry[:3], carry[3:15], carry[15:]
        after = fetch(step + 2)
        coming = look_up(words)
        for k in range(4):
            sums = add(*found[3 * k : 3 * k + 3], sums)
        return (*after, *coming, *sums)

    if carry is None:
        carry = (*fetch(jnp.int32(1)), *look_up(fetch(jnp.int32(0))))
    sums = (jnp.zeros((8, 128), F32),) * (PARTS + 1)
    begin = block * quads
    out = lax.fori_loop(begin, begin + quads, absorb, (*carry, *sums))
    return out[15:], out[:15]


def block_swap(block, regroup):
    sublane, lane = row_iota(8), lane_iota(8)
    group, place = lane >> 4, lane & 15
    skewed = lane_pick(block, ((group + sublane) & 7) * 16 + place)
    skewed = sublane_pick(skewed, (sublane - group) & 7)
    if regroup:
        y, z = lane & 15, lane >> 4
        group, place = y >> 1, (y & 1) * 8 + z
    return lane_pick(skewed, ((sublane - group) & 7) * 16 + place)


def along_y(field, k, low, high):
    y = lane_iota(16) & 15
    low = pltpu.roll(low, 128 - (4 + 4 * k), 1)
    high = pltpu.roll(high, 16 - 4 * k, 1)
    total = None
    for m in range(1, 5):
        up = pltpu.roll(jnp.where(y < m, high, field), 128 - m, 1)
        down = pltpu.roll(jnp.where(y >= 16 - m, low, field), m, 1)
        term = weights[m - 1] * (up - down)
        total = term if total is None else total + term
    return total


def along_z(field, low, high):
    z = lane_iota(16) >> 4
    total = None
    for m in range(1, 5):
        up = pltpu.roll(jnp.where(z < m, high, field), 128 - 16 * m, 1)
        down = pltpu.roll(jnp.where(z >= 8 - m, low, field), 16 * m, 1)
        term = weights[m - 1] * (up - down)
        total = term if total is None else total + term
    return total


def along_x(padded):
    total = None
    for m in range(1, 5):
        term = weights[m - 1] * (padded[8 + m : 24 + m, :] - padded[8 - m : 24 - m, :])
        total = term if total is None else total + term
    return total


class Halo:
    def __init__(self, step, refs, me):
        self.step, self.me = step, me
        self.xs, self.xl, self.xr, self.xb, self.ys, self.yr, self.zs, self.zr, send, recv = refs
        x, y, a = me
        ends = [((x + 1) % GX, y, a), ((x + GX - 1) % GX, y, a)]
        ends += [(x, (y + 1) % GY, a), (x, (y + GY - 1) % GY, a), (x, y, 1 - a)]
        i = step
        pairs = [
            (self.xs.at[i, :, 8:16], self.xl.at[i]),
            (self.xs.at[i, :, 0:8], self.xr.at[i]),
            (self.ys.at[i, 0], self.yr.at[i, 0]),
            (self.ys.at[i, 1], self.yr.at[i, 1]),
            (self.zs.at[i], self.zr.at[i]),
        ]
        self.copies = [
            pltpu.make_async_remote_copy(
                src_ref=source,
                dst_ref=target,
                send_sem=send.at[i, n],
                recv_sem=recv.at[i, n],
                device_id=end,
                device_id_type=MESH,
            )
            for n, ((source, target), end) in enumerate(zip(pairs, ends))
        ]

    def start_y(self, fields):
        self.along_y = fields
        i = self.step
        quarter = (lane_iota(16) & 15) >> 2
        for side, offset in ((0, 128 - 12), (1, 0)):
            rolled = [
                pltpu.roll(fields[k], (offset + 4 * k) % 128, 1) if offset + 4 * k else fields[k]
                for k in range(3)
            ]
            self.ys[i, side] = jnp.where(
                quarter == 0, rolled[0], jnp.where(quarter == 1, rolled[1], rolled[2])
            )
            self.copies[2 + side].start()

    def start_x(self, fields):
        self.along_x = fields
        for k in range(3):
            self.xs[self.step, k] = fields[k]
        self.copies[0].start()
        self.copies[1].start()

    def start_z(self, fields):
        self.along_z = fields
        for k in range(3):
            self.zs[self.step, k] = fields[k]
        self.copies[4].start()

    def start(self, along):
        fx, fy, fz = along
        self.start_y(fy)
        self.start_x(fx)
        self.start_z(fz)

    def finish(self):
        x, y, a = self.me
        i = self.step
        self.copies[4].wait()
        dz = []
        for k in range(3):
            other = self.zr[i, k]
            low, high = jnp.where(a > 0, other, 0.0), jnp.where(a == 0, other, 0.0)
            dz.append(along_z(self.along_z[k], low, high))
        self.copies[0].wait()
        self.copies[1].wait()
        for k in range(3):
            self.xb[k, 0:8, :] = jnp.where(x > 0, self.xl[i, k], 0.0)
            self.xb[k, 8:24, :] = self.along_x[k]
            self.xb[k, 24:32, :] = jnp.where(x < GX - 1, self.xr[i, k], 0.0)
        dx = [along_x(self.xb.at[k]) for k in range(3)]
        self.copies[2].wait()
        self.copies[3].wait()
        low = jnp.where(y > 0, self.yr[i, 0], 0.0)
        high = jnp.where(y < GY - 1, self.yr[i, 1], 0.0)
        dy = [along_y(self.along_y[k], k, low, high) for k in range(3)]
        return dx, dy, dz


def new_velocity(velocity, diffs, factor):
    dx, dy, dz = diffs
    return [velocity[k] + (dx[k] + dy[k] + dz[k]) * factor for k in range(3)]


def strain_rates(diffs):
    dx, dy, dz = diffs
    return [dx[0], dy[1], dz[2], dy[2] + dz[1], dx[2] + dz[0], dx[1] + dy[0]]


def new_component(stress, strain, stiffness, row):
    change = ordered_sum([stiffness[upper(row, col)] * strain[col] for col in range(6)])
    return stress[row] + time_step * change


def new_stress(stress, strain, stiffness):
    return [new_component(stress, strain, stiffness, row) for row in range(6)]


def stress_parts(stress):
    return tuple([stress[i] for i in which] for which in (STRESS_X, STRESS_Y, STRESS_Z))


def entries_of(parts, even):
    out = []
    for i in range(21):
        entry = sparse(FROM_PARTS[i], parts)
        if EVEN[i].any():
            constant = jnp.concatenate([even[i], even[i]], axis=0)
            entry = constant if entry is None else entry + constant
        out.append(entry)
    return out


def main_kernel(*refs):
    given, outs, refs = refs[:8], refs[8:10], refs[10:]
    held, refs = refs[:8], refs[8:]
    angles, table, seeds, even, packed, from_row, from_lane, partial = refs[:8]
    refs = refs[8:]
    fields, arrived, first, first_in, second, second_in, stiff, waves = refs[:8]
    load_sem, out_sem = refs[8:10]
    rs_send, rs_recv, p1_send, p1_recv, p2_send, p2_recv = refs[10:16]
    halo_refs = refs[16:]
    stores = [
        pltpu.make_async_copy(stiff, outs[0], out_sem.at[0]),
        pltpu.make_async_copy(waves.at[0:48], outs[1].at[0:48], out_sem.at[1]),
        pltpu.make_async_copy(waves.at[48:144], outs[1].at[48:144], out_sem.at[2]),
    ]

    loads = [pltpu.make_async_copy(given[i], held[i], load_sem.at[i]) for i in range(8)]
    for load in loads:
        load.start()
    euler, crystal, orient, weight, cell_map, density, velocity, stress = held
    x, y, a = lax.axis_index("gx"), lax.axis_index("gy"), lax.axis_index("ga")
    barrier = pltpu.get_barrier_semaphore()
    ends = [((x + d) % GX, y, a) for d in sorted(range(1, GX), key=lambda d: -min(d, GX - d))]
    ends += [(x, (y + d) % GY, a) for d in range(1, GY)]
    ends += [(x, y, 1 - a)]
    for end in ends:
        pl.semaphore_signal(barrier, inc=1, device_id=end, device_id_type=MESH)

    loads[0].wait()
    loads[1].wait()
    prepare_table(euler, crystal, angles, table, seeds, even)
    for i in range(2, 5):
        loads[i].wait()
    prepare_cells(orient, weight, cell_map, packed, from_row, from_lane)

    halos = [Halo(step, halo_refs, (x, y, a)) for step in range(2 * STEPS)]
    half = [
        pltpu.make_async_remote_copy(
            src_ref=partial.at[pl.ds(i * 8, 8), 0 : PARTS + 1],
            dst_ref=arrived.at[pl.ds(i * 8, 8), 0 : PARTS + 1],
            send_sem=rs_send.at[i],
            recv_sem=rs_recv.at[i],
            device_id=(x, y, 1 - a),
            device_id_type=MESH,
        )
        for i in range(2)
    ]
    def slot_of(d):
        return (GX - d - FIRST) % GX

    to_brick = {}
    for row in range(16):
        d = (row + NEAR) % GX
        if d:
            to_brick[row] = pltpu.make_async_remote_copy(
                src_ref=first.at[row, 0:PARTS],
                dst_ref=first_in.at[slot_of(d), 0:PARTS],
                send_sem=p1_send.at[d - 1],
                recv_sem=p1_recv.at[d - 1],
                device_id=((x + d) % GX, y, a),
                device_id_type=MESH,
            )

    carry = [None]

    def sums_of(block):
        sums, carry[0] = grain_sums(table, seeds, packed, from_row, from_lane, block, carry[0])
        return sums

    def other_half(i):
        sums = sums_of(i)
        for c in range(PARTS + 1):
            partial[i * 8 : i * 8 + 8, c, :] = sums[c]

    def own_half(i):
        sums = sums_of(2 + i)
        half[i].wait()
        rows = slice(i * 8, i * 8 + 8)
        gain = 1.0 / (sums[PARTS] + arrived[rows, PARTS, :])
        for c in range(PARTS):
            first[rows, c, :] = (sums[c] + arrived[rows, c, :]) * gain
        for row in (4, 3, 5, 2, 6, 1, 7, 0) if i == 0 else (8, 9, 15, 10, 14, 11, 13, 12):
            if row in to_brick:
                to_brick[row].start()

    other_half(0)
    for i in range(5, 8):
        loads[i].wait()
    for z in range(8):
        lanes = slice(z * 16, z * 16 + 16)
        fields[0:96, lanes] = stress[pl.ds(z, 96, stride=8), :]
        fields[96:144, lanes] = velocity[pl.ds(z, 48, stride=8), :]
        fields[144:160, lanes] = density[pl.ds(z, 16, stride=8), :]
    stresses = [fields[i * 16 : i * 16 + 16, :] for i in range(6)]
    pl.semaphore_wait(barrier, len(ends))
    half[0].start()
    halos[0].start(stress_parts(stresses))
    other_half(1)
    half[1].start()
    own_half(0)
    factor = time_step / fields[144:160, :]
    velocities = [fields[96 + k * 16 : 112 + k * 16, :] for k in range(3)]
    velocities = new_velocity(velocities, halos[0].finish(), factor)
    for k in range(3):
        fields[96 + k * 16 : 112 + k * 16, :] = velocities[k]
    fields[144:160, :] = factor
    halos[1].start((velocities,) * 3)
    own_half(1)

    to_y = []

    def forward(g):
        for c in range(PARTS):
            block = first_in[g * 8 : g * 8 + 8, c, :]
            second[:, g, c, :] = block_swap(block, False)
        for d in (6, 2, 4, 5, 3, 7, 1):
            target = (y + d) % GY
            copy = pltpu.make_async_remote_copy(
                src_ref=second.at[target, g, 0:PARTS],
                dst_ref=second_in.at[y, g, 0:PARTS],
                send_sem=p2_send.at[g * (GY - 1) + d - 1],
                recv_sem=p2_recv.at[g * (GY - 1) + d - 1],
                device_id=(x, target, a),
                device_id_type=MESH,
            )
            copy.start()
            to_y.append(copy)
        second_in[y, g, 0:PARTS, :] = second[y, g, 0:PARTS, :]

    for row in range(8):
        to_brick[row].wait()
    forward(0)
    velocities = [fields[96 + k * 16 : 112 + k * 16, :] for k in range(3)]
    halos[1].along_x = halos[1].along_y = halos[1].along_z = velocities
    strain = strain_rates(halos[1].finish())
    for i in range(6):
        fields[160 + i * 16 : 176 + i * 16, :] = strain[i]
    first_in[slot_of(0), 0:PARTS, :] = first[GX - NEAR, 0:PARTS, :]
    for row in range(8, 16):
        if row in to_brick:
            to_brick[row].wait()
    forward(1)
    for copy in to_y:
        copy.wait()
    parts = []
    for c in range(PARTS):
        rows = [block_swap(second_in[:, g, c, :], True) for g in range(2)]
        parts.append(pltpu.roll(jnp.concatenate(rows, axis=0), (x + FIRST) % GX, 0))
    for i, entry in enumerate(entries_of(parts, even)):
        stiff[i] = entry

    strain = [fields[160 + i * 16 : 176 + i * 16, :] for i in range(6)]
    stresses = [fields[i * 16 : i * 16 + 16, :] for i in range(6)]
    fresh = {}
    for which, begin in (
        (STRESS_Y, halos[2].start_y),
        (STRESS_X, halos[2].start_x),
        (STRESS_Z, halos[2].start_z),
    ):
        for row in which:
            if row not in fresh:
                fresh[row] = new_component(stresses, strain, stiff, row)
        begin([fresh[row] for row in which])
    stresses = [fresh[row] for row in range(6)]
    stores[0].start()
    factor = fields[144:160, :]
    velocities = [fields[96 + k * 16 : 112 + k * 16, :] for k in range(3)]
    velocities = new_velocity(velocities, halos[2].finish(), factor)
    halos[3].start((velocities,) * 3)
    for k in range(3):
        waves[k * 16 : k * 16 + 16, :] = velocities[k]
    stores[1].start()
    strain = strain_rates(halos[3].finish())
    stresses = new_stress(stresses, strain, stiff)
    for k in range(6):
        waves[48 + k * 16 : 64 + k * 16, :] = stresses[k]
    stores[2].start()
    for store in stores:
        store.wait()


def layout_kernel(
    stiff_in, waves_in, stiff_out, velocity_out, stress_out,
    stiff, waves, stiff_held, velocity_held, stress_held, sems, load_sems,
):
    loads = [
        pltpu.make_async_copy(waves_in, waves, load_sems.at[0]),
        pltpu.make_async_copy(stiff_in, stiff, load_sems.at[1]),
    ]
    for load in loads:
        load.start()
    loads[0].wait()
    copies = []

    def send(source, target):
        copies.append(pltpu.make_async_copy(source, target, sems.at[len(copies)]))
        copies[-1].start()

    for z in range(8):
        lanes = slice(z * 16, z * 16 + 16)
        stress_held[pl.ds(z, 96, stride=8), :] = waves[48:144, lanes]
        velocity_held[pl.ds(z, 48, stride=8), :] = waves[0:48, lanes]
    send(stress_held, stress_out)
    send(velocity_held, velocity_out)
    loads[1].wait()
    for row in range(16):
        turned = jnp.transpose(stiff[:, row, :], (1, 0))
        for z in range(8):
            stiff_held[pl.ds(row * 128 + z, 16, stride=8), :] = turned[z * 16 : z * 16 + 16, :21]
        if row % 4 == 3:
            rows = pl.ds((row - 3) * 128, 512)
            send(stiff_held.at[rows, :], stiff_out.at[rows, :])
    for copy in copies:
        copy.wait()


def on_device(euler_table, crystal, orient, weight, cell_map, density, velocity, stress):
    anywhere = pl.BlockSpec(memory_space=pl.ANY)
    operands = (
        euler_table,
        crystal,
        orient.reshape(512, 128),
        weight.reshape(GRAINS, 4096),
        cell_map.reshape(32, 128),
        density.transpose(0, 2, 1).reshape(128, 16),
        velocity.transpose(0, 1, 3, 2).reshape(384, 16),
        stress.transpose(0, 1, 3, 2).reshape(768, 16),
    )
    scratch = [
        (pltpu.SMEM if i == 1 else pltpu.VMEM)(array.shape, array.dtype)
        for i, array in enumerate(operands)
    ]
    scratch += [
        pltpu.VMEM((48, 128), F32),
        pltpu.VMEM((32, 128), I32),
        pltpu.VMEM((PARTS, 8, 128), F32),
        pltpu.VMEM((21, 8, 128), F32),
        pltpu.VMEM((512, 128), I32),
        pltpu.VMEM((32, 128), I32),
        pltpu.VMEM((32, 128), I32),
        pltpu.VMEM((16, ROWS, 128), F32),
        pltpu.VMEM((256, 128), F32),
        pltpu.VMEM((16, ROWS, 128), F32),
        pltpu.VMEM((16, ROWS, 128), F32),
        pltpu.VMEM((16, ROWS, 128), F32),
        pltpu.VMEM((8, 2, ROWS, 128), F32),
        pltpu.VMEM((8, 2, ROWS, 128), F32),
    ]
    small = (jax.ShapeDtypeStruct((21, 16, 128), F32), jax.ShapeDtypeStruct((144, 128), F32))
    small_held = [pltpu.VMEM(array.shape, F32) for array in small]
    scratch += small_held
    for count in (8, 3, 2, 2, 15, 15, 14, 14):
        scratch.append(pltpu.SemaphoreType.DMA((count,)))
    steps = 2 * STEPS
    scratch += [
        pltpu.VMEM((steps, 3, 16, 128), F32),
        pltpu.VMEM((steps, 3, 8, 128), F32),
        pltpu.VMEM((steps, 3, 8, 128), F32),
        pltpu.VMEM((3, 32, 128), F32),
        pltpu.VMEM((steps, 2, 16, 128), F32),
        pltpu.VMEM((steps, 2, 16, 128), F32),
        pltpu.VMEM((steps, 3, 16, 128), F32),
        pltpu.VMEM((steps, 3, 16, 128), F32),
        pltpu.SemaphoreType.DMA((steps, 5)),
        pltpu.SemaphoreType.DMA((steps, 5)),
    ]
    found = pl.pallas_call(
        main_kernel,
        out_shape=small,
        in_specs=[anywhere] * 8,
        out_specs=(anywhere, anywhere),
        scratch_shapes=scratch,
        compiler_params=pltpu.CompilerParams(
            collective_id=0, has_side_effects=True, vmem_limit_bytes=VMEM_LIMIT
        ),
        name="relay_and_steps",
    )(*operands)
    shapes = ((2048, 21), (384, 16), (768, 16))
    stiffness, velocity, stress = pl.pallas_call(
        layout_kernel,
        out_shape=tuple(jax.ShapeDtypeStruct(shape, F32) for shape in shapes),
        in_specs=[anywhere, anywhere],
        out_specs=(anywhere,) * 3,
        scratch_shapes=small_held
        + [pltpu.VMEM(shape, F32) for shape in shapes]
        + [pltpu.SemaphoreType.DMA((6,)), pltpu.SemaphoreType.DMA((2,))],
        compiler_params=pltpu.CompilerParams(vmem_limit_bytes=VMEM_LIMIT),
        name="layouts",
    )(*found)
    return (
        stiffness.reshape(16, 16, 8, 21).transpose(3, 0, 1, 2),
        velocity.reshape(3, 16, 8, 16).transpose(0, 1, 3, 2),
        stress.reshape(6, 16, 8, 16).transpose(0, 1, 3, 2),
    )


def solution(mesh):
    fields = P(None, "gx", "gy", "ga")
    return jax.shard_map(
        on_device,
        mesh=mesh,
        in_specs=(
            P(),
            P(),
            P("ga", "gx", "gy", None),
            P("ga", "gx", "gy", None),
            P("gx", "gy", None),
            P("gx", "gy", "ga"),
            fields,
            fields,
        ),
        out_specs=(fields, fields, fields),
        check_vma=False,
    )
```
